128 devices in a mesh: section: 8 (over y, core), space: 16 (over x, z).
Axes of the slice: x: 4, y: 4, z: 4, core: 2. Of those that a mesh axis runs over, the one named last changes fastest.
Arguments:
- features: bfloat16 [16, 4, 32, 256], P('space'), may hold values from -6 to 6
- section_weight: bfloat16 [8, 512, 27, 256], P('section'), may hold values from -0.0546875 to 0.0546875
- section_bias: float32 [8, 256], P('section'), may hold values from -2.5 to 2.5
- cotangent: bfloat16 [16, 4, 32, 256], P('space'), may hold values from -6 to 6
Outputs:
- grad_features: float32 [16, 4, 32, 256], P('space', None, None, 'section')
- grad_weight: float32 [8, 512, 27, 256], P('section', 'space')
The draws below stay inside these ranges and needn't reach their ends.
All inputs are finite; a program needn't handle non-finite values.
Results may differ from the reference program's by a relative error of at most 0.033.
Values may be sent and summed in bfloat16 or wider, within the bound.
No kernel may reach another device: no remote copies, remote signals or barrier semaphores. Data moves between devices by JAX's collectives and lax.ppermute only.
A program may use at most 128 MiB of HBM per device.

```python
import jax
import jax.numpy as jnp
from jax import lax

CH = 256
CZ = 4
CY = 32
SECTIONS = 8
NX = 16


def block_scale(rng, shape, shards, low, largest):
    level = 1.0
    for dim, shards_of in shards:
        steps = jax.random.uniform(jax.random.fold_in(jax.random.fold_in(rng, 6), dim), (shards_of,), jnp.float32, low / len(shards), largest / len(shards))
        level = level * jnp.repeat(jnp.exp(steps), shape[dim] // shards_of).reshape((-1,) + (1,) * (len(shape) - 1 - dim))
    return level


def bell_draw(own_key, dims, width, reach, shards=(), dtype=jnp.bfloat16):
    values = width * jax.random.normal(own_key, dims, jnp.float32)
    if shards:
        values = values * block_scale(own_key, dims, shards, -0.22, 0.18)
    return jnp.clip(values, -reach, reach).astype(dtype)


def setup_inputs(seed: int = 0) -> dict:
    key_list = jax.random.split(jax.random.key(seed), 5)
    features = bell_draw(key_list[0], (NX, CZ, CY, CH), 1.0, 6.0, ((0, 16),))
    section_weight = bell_draw(key_list[1], (SECTIONS, 2 * CH, 27, CH), (54 * CH) ** -0.5, 0.0546875, ((0, 8),))
    section_bias = bell_draw(key_list[2], (SECTIONS, CH), 0.5, 2.5, ((0, 8),), jnp.float32)
    cotangent = bell_draw(key_list[3], (NX, CZ, CY, CH), 0.5, 6.0, ((0, 16),))
    return {"features": features, "section_weight": section_weight, "section_bias": section_bias, "cotangent": cotangent}


def conv_cells(field, kernel, layout, pad_first):
    result = lax.conv_general_dilated(field[None], kernel, (1, 1, 1), (pad_first, (1, 1), (1, 1)), dimension_numbers=('NDHWC', layout, 'NDHWC'), preferred_element_type=jnp.float32)
    return result[0]

def weight_grad(padded, slopes):
    size_x, size_z, size_y = (slopes.shape[0], slopes.shape[1], slopes.shape[2])
    flat_slopes = slopes.reshape(-1, slopes.shape[3])
    tap_list = []
    for first in range(3):
        for second in range(3):
            for third in range(3):
                window = padded[first:first + size_x, second:second + size_z, third:third + size_y].reshape(-1, padded.shape[3])
                tap_list.append(jnp.dot(window.T, flat_slopes, preferred_element_type=jnp.float32))
    return jnp.stack(tap_list, axis=1)

def reference(features, section_weight, section_bias, cotangent):
    section_count = SECTIONS
    half_count = section_count // 2
    current = features
    joined_all = []
    preacts = []
    outputs = []
    for section in range(section_count):
        side_input = features if section < half_count else outputs[section_count - 1 - section]
        joined = jnp.concatenate([current, side_input], 3)
        kernel = section_weight[section].reshape(2 * CH, 3, 3, 3, CH)
        preact = conv_cells(joined, kernel, 'IDHWO', (1, 1)) + section_bias[section]
        output = (current.astype(jnp.float32) + jax.nn.silu(preact)).astype(jnp.bfloat16)
        joined_all.append(joined)
        preacts.append(preact)
        outputs.append(output)
        current = output
    cotan = cotangent
    skip_grads = {}
    feature_grad = jnp.zeros(features.shape, jnp.float32)
    weight_grads = [None] * section_count
    for section in reversed(range(section_count)):
        if section < half_count:
            cotan = (cotan.astype(jnp.float32) + skip_grads[section_count - 1 - section].astype(jnp.float32)).astype(jnp.bfloat16)
        preact = preacts[section]
        logistic = jax.nn.sigmoid(preact)
        slopes = (cotan.astype(jnp.float32) * logistic * (1.0 + preact * (1.0 - logistic))).astype(jnp.bfloat16)
        flipped = section_weight[section].reshape(2 * CH, 3, 3, 3, CH)[:, ::-1, ::-1, ::-1, :]
        backward = conv_cells(slopes, flipped, 'ODHWI', (1, 1))
        padded = jnp.pad(joined_all[section], ((1, 1), (1, 1), (1, 1), (0, 0)))
        weight_grads[section] = weight_grad(padded, slopes)
        if section >= half_count:
            skip_grads[section] = backward[..., CH:].astype(jnp.bfloat16)
        else:
            feature_grad = feature_grad + backward[..., CH:]
        cotan = (cotan.astype(jnp.float32) + backward[..., :CH]).astype(jnp.bfloat16)
    feature_grad = feature_grad + cotan.astype(jnp.float32)
    return (feature_grad, jnp.stack(weight_grads))
```

```python
import functools

import jax
import jax.numpy as jnp
from jax import lax
from jax.experimental import pallas as pl
from jax.experimental.pallas import tpu as pltpu
from jax.sharding import PartitionSpec as P

BF16 = jnp.bfloat16
F32 = jnp.float32
TAPS = [(a, b) for a in range(3) for b in range(3)]
VMEM = pl.BlockSpec(memory_space=pltpu.VMEM)
SMEM = pl.BlockSpec(memory_space=pltpu.SMEM)
BOTH = ("section", "space")


def fill(pad, block, row):
    zero = jnp.zeros((pad.shape[0], row, pad.shape[2]), BF16)
    pad[:, :row, :] = zero
    pad[:, pad.shape[1] - row :, :] = zero
    pad[:, row : pad.shape[1] - row, :] = block


def shift_sum(low, mid, high, row):
    rows = mid.shape[0]
    y = lax.broadcasted_iota(jnp.int32, mid.shape, 0) % row
    low = jnp.where(y == 0, 0.0, pltpu.roll(low, 1, 0))
    high = jnp.where(y == row - 1, 0.0, pltpu.roll(high, rows - 1, 0))
    return mid + low + high


def conv(pad, w_ref, offset, count, row, flip):
    ch = pad.shape[2]
    cells = pad.shape[1] - 2 * row
    parts = []
    for c in range(3):
        total = None
        for a, b in TAPS:
            lhs = pad[a : a + count, b * row : b * row + cells, :].reshape(count * cells, ch)
            if flip:
                tap = 26 - (9 * a + 3 * b + c)
                dims = (((1,), (1,)), ((), ()))
            else:
                tap = 9 * a + 3 * b + c
                dims = (((1,), (0,)), ((), ()))
            part = lax.dot_general(
                lhs, w_ref[tap, offset : offset + ch, :], dims, preferred_element_type=F32
            )
            total = part if total is None else total + part
        parts.append(total)
    return shift_sum(*parts, row).reshape(count, cells, ch)


def edge_mask(edge_ref, value):
    if value.shape[0] == 1:
        return value
    low = jnp.where(edge_ref[0] > 0, value[:1], 0.0)
    high = jnp.where(edge_ref[1] > 0, value[2:], 0.0)
    return jnp.concatenate([low, value[1:2], high], 0)


def forward_kernel(count, row, edge_ref, act_ref, w_ref, base_ref, out_ref, fac_ref, pad):
    fill(pad, act_ref[...], row)
    preact = conv(pad, w_ref, 0, count, row, False) + base_ref[...]
    logistic = jax.nn.sigmoid(preact)
    out = act_ref[1 : 1 + count].astype(F32) + preact * logistic
    out_ref[...] = edge_mask(edge_ref, out).astype(BF16)
    fac_ref[...] = edge_mask(edge_ref, logistic * (1.0 + preact * (1.0 - logistic)))


def side_kernel(row, side_ref, w_ref, bias_ref, out_ref, pad):
    fill(pad, side_ref[...], row)
    out_ref[...] = conv(pad, w_ref, pad.shape[2], 3, row, False) + bias_ref[...]


def side_back_kernel(row, slope_ref, w_ref, out_ref, pad):
    fill(pad, slope_ref[...], row)
    out_ref[...] = conv(pad, w_ref, pad.shape[2], 3, row, True).astype(BF16)


def wide_back_kernel(row, cot_ref, fac_ref, w_ref, sent_ref, slope_ref, pad):
    slope = (cot_ref[...].astype(F32) * fac_ref[...].astype(F32)).astype(BF16)
    slope_ref[...] = slope
    fill(pad, slope, row)
    back = conv(pad, w_ref, 0, 3, row, True)
    sent_ref[...] = (cot_ref[1:4].astype(F32) + back).astype(BF16)


def narrow_back_kernel(
    row, sent_in_ref, skip_ref, extra_ref, fac_ref, w_ref, sent_ref, total_ref, slope_ref, pad
):
    cot = (sent_in_ref[...].astype(F32) + skip_ref[...].astype(F32)).astype(BF16).astype(F32)
    slope = (cot * fac_ref[...]).astype(BF16)
    slope_ref[...] = slope
    fill(pad, slope, row)
    total = cot[1:2] + conv(pad, w_ref, 0, 1, row, True)
    total_ref[...] = total
    sent_ref[...] = (total + extra_ref[...].astype(F32)).astype(BF16)


def window_kernel(row, joined_ref, out_ref):
    rows, cells = joined_ref.shape
    span = 4 * row
    value = joined_ref[...].astype(F32)
    cell = lax.broadcasted_iota(jnp.int32, value.shape, 1)
    z = cell // row % 4
    y = cell % row
    zero = jnp.zeros((rows, span), BF16)
    for b in range(3):
        for c in range(3):
            move = (b - 1) * row + (c - 1)
            part = value if move == 0 else pltpu.roll(value, (-move) % cells, 1)
            valid = (z + b - 1 >= 0) & (z + b - 1 < 4) & (y + c - 1 >= 0) & (y + c - 1 < row)
            part = jnp.where(valid, part, 0.0).astype(BF16)
            out_ref[3 * b + c, :, :span] = zero
            out_ref[3 * b + c, :, span : span + cells] = part
            out_ref[3 * b + c, :, span + cells :] = zero


def weight_grad_kernel(groups, width, place_ref, window_ref, *refs):
    slope_refs, out_ref = refs[:groups], refs[groups]
    rows = window_ref.shape[1]
    span = 128
    for a in range(3):
        total = None
        for g in range(groups):
            start = pl.multiple_of(place_ref[g] * width + a * span, span)
            lhs = window_ref[:, :, pl.ds(start, width)].reshape(9 * rows, width)
            part = jnp.dot(lhs, slope_refs[g][...], preferred_element_type=F32)
            total = part if total is None else total + part
        out_ref[9 * a : 9 * a + 9] = total.reshape(9, rows, -1)


def params():
    return pltpu.CompilerParams(vmem_limit_bytes=48 * 2**20)


def shards(features, section_weight, section_bias, cotangent):
    sections = lax.axis_size("section")
    spaces = lax.axis_size("space")
    half = sections // 2
    chips = sections // 2
    section = lax.axis_index("section")
    place = lax.axis_index("space")
    chip, core = section // 2, section % 2
    _, depth, row, ch = features.shape
    cells = depth * row

    weight = jnp.transpose(section_weight[0], (1, 0, 2))
    doubled = (section == 0) | (section == half)
    weight_act = weight[:, :ch]
    weight_act = jnp.where(
        doubled, (weight_act.astype(F32) + weight[:, ch:].astype(F32)).astype(BF16), weight_act
    )
    bias = section_bias.reshape(1, 1, ch)
    edges = jnp.stack([place > 0, place < spaces - 1]).astype(jnp.int32)

    def call(kernel, outs, specs, pad_slices):
        scratch = [pltpu.VMEM((pad_slices, (depth + 2) * row, ch), BF16)] if pad_slices else []
        return pl.pallas_call(
            kernel,
            out_shape=[jax.ShapeDtypeStruct(s, t) for s, t in outs],
            in_specs=specs,
            out_specs=[VMEM] * len(outs),
            scratch_shapes=scratch,
            compiler_params=params(),
        )

    def forward(count, act, base):
        shape = (count, cells, ch)
        return call(
            functools.partial(forward_kernel, count, row),
            [(shape, BF16), (shape, F32)],
            [SMEM, VMEM, VMEM, VMEM],
            count + 2,
        )(edges, act, weight_act, base)

    def side_part(side):
        return call(
            functools.partial(side_kernel, row), [((3, cells, ch), F32)], [VMEM] * 3, 5
        )(side, weight, bias)[0]

    def side_back(slope):
        return call(
            functools.partial(side_back_kernel, row), [((3, cells, ch), BF16)], [VMEM] * 2, 5
        )(slope, weight)[0]

    def wide_back(cot, fac):
        return call(
            functools.partial(wide_back_kernel, row),
            [((3, cells, ch), BF16), ((5, cells, ch), BF16)],
            [VMEM] * 3,
            5,
        )(cot, fac, weight_act)

    def narrow_back(sent, skip, extra, fac):
        return call(
            functools.partial(narrow_back_kernel, row),
            [((1, cells, ch), BF16), ((1, cells, ch), F32), ((3, cells, ch), BF16)],
            [VMEM] * 5,
            3,
        )(sent, skip, extra, fac, weight_act)

    def sibling(block):
        return lax.ppermute(block, "section", [(s, s ^ 1) for s in range(sections)])

    def neighbours(block):
        moved = {
            d: lax.ppermute(block, "space", [(x, (x + d) % spaces) for x in range(spaces)])
            for d in (2, -2, 1, -1)
        }
        return jnp.concatenate([moved[2], moved[1], block, moved[-1], moved[-2]], 0)

    def hop(block, source, target):
        moved = {
            d: lax.ppermute(
                block,
                BOTH,
                [
                    (source * spaces + x, target * spaces + x + d)
                    for x in range(spaces)
                    if 0 <= x + d < spaces
                ],
            )
            for d in (2, -2, 1, -1, 0)
        }
        return jnp.concatenate([moved[d] for d in (2, 1, 0, -1, -2)], 0)

    def along(block, *pairs):
        return lax.ppermute(block, "section", pairs)

    x = place + jnp.arange(-2, 3)
    inside = ((x >= 0) & (x < spaces)).reshape(5, 1, 1)

    own = features.reshape(1, cells, ch)
    features5 = jnp.where(inside, neighbours(own), 0)
    base = jnp.broadcast_to(bias, (3, cells, ch))

    act5 = features5
    act5_all, in3_all, out3_all, fac3_all, fac1_all = [], [], [], [], []
    base3 = None
    for k in range(chips):
        if k == 0:
            base_a = base
        elif k == chips // 2:
            base_a = base
        else:
            base_a = base3
        out3, fac3 = forward(3, act5, base_a)
        in3 = sibling(out3)
        if k == 0:
            base3 = side_part(features5)
            cot5 = jnp.where(inside, neighbours(cotangent.reshape(1, cells, ch)), 0)
        act5_all.append(act5)
        in3_all.append(in3)
        out3_all.append(out3)
        fac3_all.append(fac3)
        out1, fac1 = forward(1, in3, base3[1:2])
        fac1_all.append(fac1)
        if k == 1:
            moved3 = along(jnp.where(section == 0, out3_all[0], out3), (0, 7), (2, 5))
            moved5 = along(act5, (2, 6))
            late = jnp.where(
                section == 6, moved5, jnp.pad(moved3, ((1, 1), (0, 0), (0, 0)))
            )
            base3_late = side_part(late)
        if k + 1 < chips:
            act5 = hop(out1, 2 * k + 1, 2 * k + 2)
            if k == 1:
                base3 = base3_late

    def mine(values):
        return lax.select_n(chip, *values)

    fac5 = neighbours(mine(fac1_all).astype(BF16))
    fac3 = mine(fac3_all)
    act_centre = jnp.where(
        core == 0, mine([v[2] for v in act5_all]), mine([v[1] for v in in3_all])
    )
    side_centre = jnp.where(
        section < half, own[0], jnp.where(section == half, act_centre, late[2])
    )

    slopes = []
    zero3 = jnp.zeros((3, cells, ch), BF16)
    skip3, extra = zero3, zero3[:1]
    for k in reversed(range(chips)):
        sent3, slope5 = wide_back(cot5, fac5)
        sent1, total, slope3 = narrow_back(sibling(sent3), skip3, extra, fac3)
        slope5 = jnp.where(core == 1, slope5, jnp.pad(slope3, ((1, 1), (0, 0), (0, 0))))
        slopes.append(slope5)
        if k > 0:
            cot5 = hop(sent1, 2 * k, 2 * k - 1)
        if k == 3:
            back_7_6 = side_back(slope5)
            moved_7_6 = along(back_7_6, (7, 0), (6, 2))
            joined = jnp.concatenate([act_centre, side_centre], 1)
            blocks = jnp.transpose(joined.reshape(cells, spaces, -1), (1, 0, 2))
            blocks = lax.all_to_all(blocks, "space", 0, 0, tiled=True)
            blocks = jnp.transpose(blocks.reshape(spaces * cells, -1))
            window = call(
                functools.partial(window_kernel, row),
                [((9, blocks.shape[0], (spaces + 2) * cells), BF16)],
                [VMEM],
                0,
            )(blocks)[0]
            cot5, window = lax.optimization_barrier((cot5, window))
        if k == 2:
            back_5 = side_back(slope5)
            moved_5 = along(back_5, (5, 2))
            skip3 = jnp.where(section == 2, moved_5, jnp.where(section == 0, moved_7_6, 0))
            extra = jnp.where(section == 2, moved_7_6[1:2], 0)
    slope5 = mine(slopes[::-1])
    own_side = side_back(slope5)[1].astype(F32)
    feature_term = jnp.where(
        section == 0, total[0], jnp.where(section < half, own_side, 0.0)
    )
    grad_features = lax.psum_scatter(
        feature_term.astype(BF16), "section", scatter_dimension=1, tiled=True
    ).astype(F32)

    inner = place % 4
    outer = place // 4
    pair = lax.dynamic_slice_in_dim(slope5, 2 - inner % 2, 2, axis=0)
    other = lax.ppermute(pair, "space", [(i, i ^ 3) for i in range(spaces)])
    group = jnp.where(
        inner < 2, jnp.concatenate([pair, other], 0), jnp.concatenate([other, pair], 0)
    )
    groups = [group] + [
        lax.ppermute(group, "space", [(i, (i + 4 * d) % spaces) for i in range(spaces)])
        for d in (2, 1, 3)
    ]
    places = jnp.stack([(outer - d) % 4 for d in (0, 2, 1, 3)]).astype(jnp.int32)
    grad_weight = call(
        functools.partial(weight_grad_kernel, 4, 4 * cells),
        [((27, window.shape[1], ch), F32)],
        [SMEM] + [VMEM] * 5,
        0,
    )(places, window, *[g.reshape(4 * cells, ch) for g in groups])[0]
    return (
        grad_features.reshape(1, depth, row, -1),
        jnp.transpose(grad_weight, (1, 0, 2))[None],
    )


def solution(mesh):
    return jax.shard_map(
        shards,
        mesh=mesh,
        in_specs=(
            P("space", None, None, None),
            P("section", None, None, None),
            P("section", None),
            P("space", None, None, None),
        ),
        out_specs=(P("space", None, None, "section"), P("section", "space", None, None)),
        check_vma=False,
    )
```

```python
import functools

import jax
import jax.numpy as jnp
from jax import lax
from jax.experimental import pallas as pl
from jax.experimental.pallas import tpu as pltpu
from jax.sharding import PartitionSpec as P

BF16 = jnp.bfloat16
F32 = jnp.float32
TAPS = [(a, b) for a in range(3) for b in range(3)]
BOTH = ("section", "space")
CORE, CHIP, LOW, HIGH = 0, 1, 2, 5


def fill(pad, info, slices, count, row):
    zero = jnp.zeros((pad.shape[0], row, pad.shape[2]), BF16)
    pad[:, :row, :] = zero
    pad[:, pad.shape[1] - row :, :] = zero
    first = 1 if count == 1 else 0
    for j in range(count):
        low = info[LOW + first + j] > 0
        high = info[HIGH + first + j] > 0
        values = [
            jnp.where(low, slices[j], jnp.zeros_like(slices[j])),
            slices[j + 1],
            jnp.where(high, slices[j + 2], jnp.zeros_like(slices[j])),
        ]
        for a in range(3):
            pad[a * count + j, row : pad.shape[1] - row, :] = values[a]


def shift_sum(low, mid, high, row):
    rows = mid.shape[0]
    y = lax.broadcasted_iota(jnp.int32, mid.shape, 0) % row
    low = jnp.where(y == 0, 0.0, pltpu.roll(low, 1, 0))
    high = jnp.where(y == row - 1, 0.0, pltpu.roll(high, rows - 1, 0))
    return mid + low + high


def taps_of(pad, first, w_ref, c, taps, count, row, flip):
    ch = pad.shape[2]
    cells = pad.shape[1] - 2 * row
    total = None
    for a, b in taps:
        lhs = pad[pl.ds(first + a * count, count), b * row : b * row + cells, :]
        tap = 9 * a + 3 * b + c
        if flip:
            tap = w_ref.shape[0] - 1 - tap
        part = lax.dot_general(
            lhs.reshape(count * cells, ch),
            w_ref[tap],
            (((1,), (1 if flip else 0,)), ((), ())),
            preferred_element_type=F32,
        )
        total = part if total is None else total + part
    return total


def conv(pad, w_ref, count, row, flip):
    parts = [taps_of(pad, 0, w_ref, c, TAPS, count, row, flip) for c in range(3)]
    return shift_sum(*parts, row).reshape(count, -1, pad.shape[2])


def forward_kernel(count, k, row, info, *refs):
    cut = 5 if count == 3 else 1
    slices, refs = refs[:cut], refs[cut:]
    w_ref, base_ref, refs = refs[0], refs[1], refs[2:]
    if k:
        (fac_old, act_old), refs = refs[:2], refs[2:]
    out_ref, fac_ref, act_ref, pad = refs
    values = [s[0] for s in slices] if count == 3 else [slices[0][i] for i in range(3)]
    fill(pad, info, values, count, row)
    base = base_ref[...]
    if count == 1 and base.shape[0] == 3:
        base = base[1:2]
    preact = conv(pad, w_ref, count, row, False) + base
    logistic = jax.nn.sigmoid(preact)
    act = jnp.stack(values[1 : 1 + count])
    out_ref[...] = (act.astype(F32) + preact * logistic).astype(BF16)
    fac = (logistic * (1.0 + preact * (1.0 - logistic))).astype(BF16)
    centre = values[2:3] if count == 3 else values[1:2]
    act = centre[0][None]
    if k:
        own = info[CHIP] == k
        fac = jnp.where(own, fac, fac_old[...])
        act = jnp.where(own, act, act_old[...])
    fac_ref[...] = fac
    act_ref[...] = act


def wide_back_kernel(k, last, row, info, *refs):
    cots, facs, refs = refs[:5], refs[5:10], refs[10:]
    skip_ref, fac_ref, w_ref, refs = refs[0], refs[1], refs[2], refs[3:]
    if not last:
        (slope_old, even_old), refs = refs[:2], refs[2:]
    send_ref, slope_ref, even_ref, pad = refs
    cot = [c[0].astype(F32) for c in cots]
    slope = [(c * f[0].astype(F32)).astype(BF16) for c, f in zip(cot, facs)]
    fill(pad, info, slope, 3, row)
    sent = (jnp.stack(cot[1:4]) + conv(pad, w_ref, 3, row, True)).astype(BF16)
    cot_even = (sent.astype(F32) + skip_ref[...].astype(F32)).astype(BF16)
    even = (cot_even.astype(F32) * fac_ref[...].astype(F32)).astype(BF16)
    send_ref[:3] = even
    send_ref[3:] = cot_even[1:2]
    slope = jnp.stack(slope)
    if not last:
        own = info[CHIP] == k
        slope = jnp.where(own, slope, slope_old[...])
        even = jnp.where(own, even, even_old[...])
    slope_ref[...] = slope
    even_ref[...] = even


def narrow_back_kernel(k, last, row, info, *refs):
    got_ref, extra_ref, w_ref, refs = refs[0], refs[1], refs[2], refs[3:]
    if not last:
        (slope_old, sent_old), refs = refs[:2], refs[2:]
    sent_ref, total_ref, slope_ref, kept_ref, pad = refs
    fill(pad, info, [got_ref[i] for i in range(3)], 1, row)
    total = got_ref[3:].astype(F32) + conv(pad, w_ref, 1, row, True)
    sent = (total + extra_ref[...].astype(F32)).astype(BF16)
    total_ref[...] = total
    sent_ref[...] = sent
    slope = got_ref[:3]
    if not last:
        own = info[CHIP] == k
        slope = jnp.where(own, slope, slope_old[...])
        sent = jnp.where(own, sent, sent_old[...])
    slope_ref[...] = slope
    kept_ref[...] = sent


def side_step(values, finish, row, flip, info, w_ref, pad, parts):
    a = pl.program_id(0)

    @pl.when(a == 0)
    def _():
        fill(pad, info, values(), 3, row)

    new = [taps_of(pad, 3 * a, w_ref, c, TAPS[:3], 3, row, flip) for c in range(3)]

    @pl.when(a == 0)
    def _():
        for c in range(3):
            parts[c] = new[c]

    @pl.when(a > 0)
    def _():
        for c in range(3):
            parts[c] = parts[c] + new[c]

    @pl.when(a == 2)
    def _():
        finish(shift_sum(parts[0], parts[1], parts[2], row).reshape(3, -1, pad.shape[2]))


def side_kernel(row, early, info, *refs):
    count = 5 if early else 1
    sides, (w_ref, bias_ref, out_ref, pad, parts) = refs[:count], refs[count:]

    def values():
        if not early:
            return [sides[0][i] for i in range(5)]
        got = [s[0] for s in sides]
        return [jnp.where(info[CORE] == 0, got[i], got[4 - i]) for i in range(5)]

    def finish(value):
        out_ref[...] = value + bias_ref[...]

    side_step(values, finish, row, False, info, w_ref, pad, parts)


def side_back_kernel(row, info, odd_ref, even_ref, w_ref, out_ref, pad, parts):
    def values():
        zero = jnp.zeros_like(even_ref[0])
        even = [zero, even_ref[0], even_ref[1], even_ref[2], zero]
        return [jnp.where(info[CORE] == 1, odd_ref[i], even[i]) for i in range(5)]

    def finish(value):
        out_ref[...] = value.astype(BF16)

    side_step(values, finish, row, True, info, w_ref, pad, parts)


def window_kernel(row, joined_ref, out_ref):
    cells = joined_ref.shape[2]
    cell = lax.broadcasted_iota(jnp.int32, joined_ref.shape[1:], 1)
    z = cell // row % 4
    y = cell % row
    for a in range(3):
        value = joined_ref[a].astype(F32)
        for b, c in TAPS:
            move = (b - 1) * row + (c - 1)
            part = value if move == 0 else pltpu.roll(value, (-move) % cells, 1)
            valid = (z + b - 1 >= 0) & (z + b - 1 < 4) & (y + c - 1 >= 0) & (y + c - 1 < row)
            out_ref[9 * a + 3 * b + c] = jnp.where(valid, part, 0.0).astype(BF16)


def weight_grad_kernel(counts, info, window_ref, *refs):
    out_ref = refs[-1]
    taps, rows, cells = window_ref.shape
    start = 0
    for kind, count in enumerate(counts):
        pieces = refs[start : start + count]
        start += count

        @pl.when(info[0] == kind)
        def _():
            slopes = jnp.concatenate([p[...].reshape(-1, p.shape[2]) for p in pieces], 0)
            for a in range(3):
                lhs = window_ref[9 * a : 9 * a + 9].reshape(9 * rows, cells)
                grad = jnp.dot(lhs, slopes, preferred_element_type=F32)
                out_ref[9 * a : 9 * a + 9] = grad.reshape(9, rows, -1)


def shards(features, section_weight, section_bias, cotangent):
    sections = lax.axis_size("section")
    spaces = lax.axis_size("space")
    half = sections // 2
    chips = sections // 2
    section = lax.axis_index("section")
    place = lax.axis_index("space")
    chip, core = section // 2, section % 2
    _, depth, row, ch = features.shape
    cells = depth * row

    weight = jnp.transpose(section_weight[0], (1, 0, 2))
    doubled = (section == 0) | (section == half)
    weight_act = weight[:, :ch]
    weight_act = jnp.where(
        doubled, (weight_act.astype(F32) + weight[:, ch:].astype(F32)).astype(BF16), weight_act
    )
    bias = section_bias.reshape(1, 1, ch)
    at = (place + jnp.arange(-1, 2)) % spaces
    info = jnp.concatenate(
        [jnp.stack([core, chip]), (at > 0), (at < spaces - 1)]
    ).astype(jnp.int32)
    vmem = pl.BlockSpec(memory_space=pltpu.VMEM)
    smem = pl.BlockSpec(memory_space=pltpu.SMEM)

    def call(kernel, ins, outs, pads, side=None):
        specs = [smem] + [vmem] * (len(ins) - 1)
        scratch = [pltpu.VMEM((pads, (depth + 2) * row, ch), BF16)] if pads else []
        extra = {}
        if side is not None:
            index, order = side
            specs[index] = pl.BlockSpec((9, ch, ch), lambda a: (order(a), 1, 0))
            scratch.append(pltpu.VMEM((3, 3 * cells, ch), F32))
            extra = {"grid": (3,)}
        return pl.pallas_call(
            kernel,
            out_shape=[jax.ShapeDtypeStruct((n, cells, ch), t) for n, t in outs]
            if isinstance(outs, list)
            else outs,
            in_specs=specs,
            out_specs=[vmem] * len(outs) if isinstance(outs, list) else vmem,
            scratch_shapes=scratch,
            compiler_params=pltpu.CompilerParams(vmem_limit_bytes=48 * 2**20),
            **extra,
        )(*ins)

    def forward(count, k, slices, base, old):
        return call(
            functools.partial(forward_kernel, count, k, row),
            [info, *slices, weight_act, base, *old],
            [(count, BF16), (count, BF16), (1, BF16)],
            3 * count,
        )

    def wide_back(k, cots, facs, skip, fac, old):
        return call(
            functools.partial(wide_back_kernel, k, not old, row),
            [info, *cots, *facs, skip, fac, weight_act, *old],
            [(4, BF16), (5, BF16), (3, BF16)],
            9,
        )

    def narrow_back(k, got, extra, old):
        return call(
            functools.partial(narrow_back_kernel, k, not old, row),
            [info, got, extra, weight_act, *old],
            [(1, BF16), (1, F32), (3, BF16), (1, BF16)],
            3,
        )

    def side_part(sides):
        return call(
            functools.partial(side_kernel, row, len(sides) == 5),
            [info, *sides, weight, bias],
            [(3, F32)],
            9,
            (1 + len(sides), lambda a: a),
        )[0]

    def side_back(odd, even):
        return call(
            functools.partial(side_back_kernel, row),
            [info, odd, even, weight],
            [(3, BF16)],
            9,
            (3, lambda a: 2 - a),
        )[0]

    def sibling(block):
        return lax.ppermute(block, "section", [(s, s ^ 1) for s in range(sections)])

    def around(block, d):
        return lax.ppermute(block, "space", [(i, (i + d) % spaces) for i in range(spaces)])

    def across(block, d, *pairs):
        route = [
            (s * spaces + i, t * spaces + (i + d) % spaces) for s, t in pairs for i in range(spaces)
        ]
        return lax.ppermute(block, BOTH, route)

    def hop(block, source, target):
        moved = {d: across(block, d, (source, target)) for d in (2, -2, 1, -1, 0)}
        return [moved[d] for d in (2, 1, 0, -1, -2)]

    def along(block, *pairs):
        return lax.ppermute(block, "section", pairs)

    def after(value, *others):
        return lax.optimization_barrier((value, *others))[0]

    own = features.reshape(1, cells, ch)
    got = []
    for d in (2, 1):
        route = []
        for s in range(sections):
            move = d if s % 2 == 0 else -d
            route += [(s * spaces + i, s * spaces + (i + move) % spaces) for i in range(spaces)]
        got.append(lax.ppermute(own, BOTH, route))
    other = [sibling(g) for g in got]
    act = [got[0], got[1], own, other[1], other[0]]
    features5 = act

    fac3 = act3 = fac1 = act1 = None
    base3 = bias
    for k in range(chips):
        old = [] if k == 0 else [fac3, act3]
        out3, fac3, act3 = forward(3, k, act, bias if k in (0, half // 2) else base3, old)
        in3 = sibling(out3)
        if k == chips - 1:
            fac_even = sibling(fac3)
        if k == 0:
            base3 = side_part(features5)
            first3 = out3
        old = [] if k == 0 else [fac1, act1]
        out1, fac1, act1 = forward(1, k, [in3], base3, old)
        if k + 1 < chips:
            act2 = act
            act = hop(out1, 2 * k + 1, 2 * k + 2)
        if k == 0:
            mine = after(cotangent.reshape(1, cells, ch), out1)
            cot = {d: across(mine, d, (7, 7)) for d in (2, -2, 1, -1)}
            cot = [cot[2], cot[1], mine, cot[-1], cot[-2]]
        if k == 1:
            moved3 = along(after(jnp.where(section == 0, first3, out3), out1), (0, 7), (2, 5))
            moved5 = along(jnp.concatenate(after((*act2, out1))[:5], 0), (2, 6))
            late = jnp.where(section == 6, moved5, jnp.pad(moved3, ((1, 1), (0, 0), (0, 0))))
            base3 = side_part([late])
    side_own = jnp.where(
        section < half, own, jnp.where(section == half, act3, late[2:3])
    )
    act_own = jnp.where(core == 0, act3, act1)

    moved = {d: around(fac1, d) for d in (2, -2, 1, -1)}
    facs = [moved[2], moved[1], fac1, moved[-1], moved[-2]]
    skip3 = jnp.zeros((3, cells, ch), BF16)
    extra = skip3[:1]
    slope5 = even3 = slope3 = kept = None
    for k in reversed(range(chips)):
        old = [] if slope5 is None else [slope5, even3]
        send, slope5, even3 = wide_back(k, cot, facs, skip3, fac_even, old)
        if k:
            got = sibling(send)
        else:
            got = along(send, (1, 0))
            evens = {d: across(even3, d, *[(q, q - 1) for q in (1, 3, 5, 7)]) for d in (3, -3, 6, -6)}
            evens[8] = across(even3[1:2], 8, *[(q, q - 1) for q in (1, 3, 5, 7)])
        old = [] if slope3 is None else [slope3, kept]
        sent, total, slope3, kept = narrow_back(k, got, extra, old)
        if k:
            cot = hop(sent, 2 * k, 2 * k - 1)
        if k == 3:
            fac_next = along(after(fac1, sent), (1, 2), (3, 4), (5, 6))
            back = side_back(after(slope5, sent), slope3)
            moved_7_6 = along(back, (7, 1), (6, 2))
            joined = after(jnp.concatenate([act_own[0], side_own[0]], 1), sent)
            blocks = jnp.transpose(joined.reshape(cells, spaces, -1), (1, 0, 2))
            blocks = lax.all_to_all(blocks, "space", 0, 0, tiled=True)
            blocks = blocks.reshape(spaces, cells, -1)
            zero = jnp.zeros_like(blocks[:1])
            shifted = jnp.stack(
                [
                    jnp.concatenate([zero, blocks[:-1]], 0),
                    blocks,
                    jnp.concatenate([blocks[1:], zero], 0),
                ]
            )
            start = (place - 1 - core) % spaces
            shifted = lax.dynamic_slice_in_dim(
                jnp.concatenate([shifted, shifted], 1), start, spaces, axis=1
            )
            shifted = jnp.transpose(shifted.reshape(3, spaces * cells, -1), (0, 2, 1))
            window = call(
                functools.partial(lambda r, i, *refs: window_kernel(r, *refs), row),
                [info, shifted],
                jax.ShapeDtypeStruct((27, shifted.shape[1], spaces * cells), BF16),
                0,
            )
            cot = list(lax.optimization_barrier((*cot, window, moved_7_6))[:5])
        if k == 2:
            back = side_back(after(slope5, sent), slope3)
            moved_5 = along(back, (5, 3))
            skip3 = jnp.where(section == 3, moved_5, jnp.where(section == 1, moved_7_6, 0))
            extra = jnp.where(section == 2, moved_7_6[1:2], 0)
        if k == 1:
            odd1 = (kept.astype(F32) * fac_next.astype(F32)).astype(BF16)
            odds = {d: across(odd1, d, (2, 1), (4, 3), (6, 5)) for d in range(3, 14)}
            whole = after(slope5, sent)
            sevens = {d: across(whole, d, (7, 7)) for d in (5, -5)}
            sevens[8] = across(whole[2:3], 8, (7, 7))

    own_side = side_back(slope5, slope3)[1]
    from_next = along(own_side, (3, 1), (2, 0)).astype(F32)
    own_term = jnp.where(section == 0, total[0], own_side.astype(F32))
    term = (own_term + from_next).astype(BF16)
    width = ch // chips
    pieces = [term[:, j * width : (j + 1) * width] for j in range(chips)]
    piece = pieces[0]
    for j in (2, 1, 3):
        moved = along(pieces[j], (0, 2 * j), (1, 2 * j + 1))
        piece = jnp.where(chip == j, moved, piece)
    lower, upper = piece[:, : width // 2], piece[:, width // 2 :]
    moved = sibling(jnp.where(core == 0, upper, lower))
    grad_features = jnp.where(core == 0, lower, upper).astype(F32) + moved.astype(F32)

    even_pieces = [slope3, evens[-3], evens[-6], evens[8], evens[6], evens[3]]
    odd_pieces = [slope5] + [odds[d] for d in range(13, 2, -1)]
    last_pieces = [slope5, sevens[-5], sevens[8], sevens[5]]
    kind = jnp.where(section == sections - 1, 2, core).astype(jnp.int32).reshape(1)
    grad_weight = call(
        functools.partial(weight_grad_kernel, [len(even_pieces), len(odd_pieces), len(last_pieces)]),
        [kind, window, *even_pieces, *odd_pieces, *last_pieces],
        jax.ShapeDtypeStruct((27, window.shape[1], ch), F32),
        0,
    )
    return (
        grad_features.reshape(1, depth, row, -1),
        jnp.transpose(grad_weight, (1, 0, 2))[None],
    )


def solution(mesh):
    return jax.shard_map(
        shards,
        mesh=mesh,
        in_specs=(
            P("space", None, None, None),
            P("section", None, None, None),
            P("section", None),
            P("space", None, None, None),
        ),
        out_specs=(P("space", None, None, "section"), P("section", "space", None, None)),
        check_vma=False,
    )
```

```python
import functools

import jax
import jax.numpy as jnp
from jax import lax
from jax.experimental import pallas as pl
from jax.experimental.pallas import tpu as pltpu
from jax.sharding import PartitionSpec as P

BF16 = jnp.bfloat16
F32 = jnp.float32
TAPS = [(a, b) for a in range(3) for b in range(3)]
BOTH = ("section", "space")
CORE, SECTION, LOW, HIGH = 0, 1, 2, 5


def fill(pad, info, slices, count, row):
    zero = jnp.zeros((pad.shape[0], row, pad.shape[2]), BF16)
    pad[:, :row, :] = zero
    pad[:, pad.shape[1] - row :, :] = zero
    first = 1 if count == 1 else 0
    for j in range(count):
        low = info[LOW + first + j] > 0
        high = info[HIGH + first + j] > 0
        values = [
            jnp.where(low, slices[j], jnp.zeros_like(slices[j])),
            slices[j + 1],
            jnp.where(high, slices[j + 2], jnp.zeros_like(slices[j])),
        ]
        for a in range(3):
            pad[a * count + j, row : pad.shape[1] - row, :] = values[a]


def shift_sum(low, mid, high, row):
    rows = mid.shape[0]
    y = lax.broadcasted_iota(jnp.int32, mid.shape, 0) % row
    low = jnp.where(y == 0, 0.0, pltpu.roll(low, 1, 0))
    high = jnp.where(y == row - 1, 0.0, pltpu.roll(high, rows - 1, 0))
    return mid + low + high


def taps_of(pad, first, w_ref, c, taps, count, row, flip):
    ch = pad.shape[2]
    cells = pad.shape[1] - 2 * row
    total = None
    for a, b in taps:
        lhs = pad[pl.ds(first + a * count, count), b * row : b * row + cells, :]
        tap = 9 * a + 3 * b + c
        if flip:
            tap = w_ref.shape[0] - 1 - tap
        part = lax.dot_general(
            lhs.reshape(count * cells, ch),
            w_ref[tap],
            (((1,), (1 if flip else 0,)), ((), ())),
            preferred_element_type=F32,
        )
        total = part if total is None else total + part
    return total


def conv(pad, w_ref, count, row, flip):
    parts = [taps_of(pad, 0, w_ref, c, TAPS, count, row, flip) for c in range(3)]
    return shift_sum(*parts, row).reshape(count, -1, pad.shape[2])


def forward_kernel(count, k, row, info, *refs):
    cut = 5 if count == 3 else 1
    slices, refs = refs[:cut], refs[cut:]
    w_ref, base_ref, refs = refs[0], refs[1], refs[2:]
    old, refs = refs[: 2 if k else 0], refs[2 if k else 0 :]
    out_ref, fac_ref, act_ref, pad = refs
    own = info[SECTION] == 2 * k + (0 if count == 3 else 1)

    @pl.when(own)
    def _():
        values = [s[0] for s in slices] if count == 3 else [slices[0][i] for i in range(3)]
        fill(pad, info, values, count, row)
        base = base_ref[...]
        if count == 1 and base.shape[0] == 3:
            base = base[1:2]
        preact = conv(pad, w_ref, count, row, False) + base
        logistic = jax.nn.sigmoid(preact)
        act = jnp.stack(values[1 : 1 + count]).astype(F32)
        out_ref[...] = (act + preact * logistic).astype(BF16)
        fac_ref[...] = (logistic * (1.0 + preact * (1.0 - logistic))).astype(BF16)
        act_ref[0] = values[2] if count == 3 else values[1]

    @pl.when(jnp.logical_not(own))
    def _():
        fac_ref[...] = old[0][...] if k else jnp.zeros_like(fac_ref)
        act_ref[...] = old[1][...] if k else jnp.zeros_like(act_ref)
        out_ref[...] = jnp.zeros_like(out_ref)


def wide_back_kernel(k, first, row, info, *refs):
    cots, facs, refs = refs[:5], refs[5:10], refs[10:]
    skip_ref, fac_ref, even_old, w_ref, refs = refs[0], refs[1], refs[2], refs[3], refs[4:]
    old, refs = refs[: 0 if first else 1], refs[0 if first else 1 :]
    send_ref, slope_ref, even_ref, pad = refs
    own = info[SECTION] == 2 * k + 1

    @pl.when(own)
    def _():
        cot = [c[0].astype(F32) for c in cots]
        slope = [(c * f[0].astype(F32)).astype(BF16) for c, f in zip(cot, facs)]
        fill(pad, info, slope, 3, row)
        sent = (jnp.stack(cot[1:4]) + conv(pad, w_ref, 3, row, True)).astype(BF16)
        cot_even = (sent.astype(F32) + skip_ref[...].astype(F32)).astype(BF16)
        send_ref[...] = cot_even
        even_ref[...] = (cot_even.astype(F32) * fac_ref[...].astype(F32)).astype(BF16)
        slope_ref[...] = jnp.stack(slope)

    @pl.when(jnp.logical_not(own))
    def _():
        send_ref[...] = jnp.zeros_like(send_ref)
        slope_ref[...] = jnp.zeros_like(slope_ref) if first else old[0][...]
        even_ref[...] = even_old[...]


def narrow_back_kernel(k, first, row, info, *refs):
    got_ref, skip_ref, extra_ref, fac_ref, w_ref, refs = *refs[:5], refs[5:]
    old, refs = refs[: 0 if first else 1], refs[0 if first else 1 :]
    sent_ref, total_ref, slope_ref, pad = refs
    own = info[SECTION] == 2 * k

    @pl.when(own)
    def _():
        cot = (got_ref[...].astype(F32) + skip_ref[...].astype(F32)).astype(BF16).astype(F32)
        slope = (cot * fac_ref[...].astype(F32)).astype(BF16)
        slope_ref[...] = slope
        fill(pad, info, [slope[i] for i in range(3)], 1, row)
        total = cot[1:2] + conv(pad, w_ref, 1, row, True)
        total_ref[...] = total
        sent_ref[...] = (total + extra_ref[...].astype(F32)).astype(BF16)

    @pl.when(jnp.logical_not(own))
    def _():
        sent_ref[...] = jnp.zeros_like(sent_ref)
        total_ref[...] = jnp.zeros_like(total_ref)
        slope_ref[...] = jnp.zeros_like(slope_ref) if first else old[0][...]


def side_conv(values, flip, row, info, w_hbm, pad, w_ref, sems):
    ch = pad.shape[2]
    copies = []
    for i in range(3):
        taps = pl.ds(9 * i, 9)
        copy = pltpu.make_async_copy(w_hbm.at[taps, pl.ds(ch, ch)], w_ref.at[taps], sems.at[i])
        copies.append(copy)
    for i in (2, 1, 0) if flip else (0, 1, 2):
        copies[i].start()
    fill(pad, info, values, 3, row)
    parts = [None] * 3
    for a in range(3):
        copies[2 - a if flip else a].wait()
        for c in range(3):
            taps = [(a, b) for b in range(3)]
            part = taps_of(pad, 0, w_ref, c, taps, 3, row, flip)
            parts[c] = part if parts[c] is None else parts[c] + part
    return shift_sum(*parts, row).reshape(3, -1, ch)


def side_kernel(row, early, info, *refs):
    count = 5 if early else 1
    sides, (w_hbm, bias_ref, out_ref, pad, w_ref, sems) = refs[:count], refs[count:]
    if early:
        got = [s[0] for s in sides]
        values = [jnp.where(info[CORE] == 0, got[i], got[4 - i]) for i in range(5)]
    else:
        values = [sides[0][i] for i in range(5)]
    out_ref[...] = side_conv(values, False, row, info, w_hbm, pad, w_ref, sems) + bias_ref[...]


def side_back_kernel(row, info, odd_ref, even_ref, w_hbm, out_ref, pad, w_ref, sems):
    zero = jnp.zeros_like(even_ref[0])
    even = [zero, even_ref[0], even_ref[1], even_ref[2], zero]
    values = [jnp.where(info[CORE] == 1, odd_ref[i], even[i]) for i in range(5)]
    out_ref[...] = side_conv(values, True, row, info, w_hbm, pad, w_ref, sems).astype(BF16)


def window_kernel(row, joined_ref, out_ref):
    cells = joined_ref.shape[2]
    cell = lax.broadcasted_iota(jnp.int32, joined_ref.shape[1:], 1)
    z = cell // row % 4
    y = cell % row
    for a in range(3):
        value = joined_ref[a].astype(F32)
        for b, c in TAPS:
            move = (b - 1) * row + (c - 1)
            part = value if move == 0 else pltpu.roll(value, (-move) % cells, 1)
            valid = (z + b - 1 >= 0) & (z + b - 1 < 4) & (y + c - 1 >= 0) & (y + c - 1 < row)
            out_ref[9 * a + 3 * b + c] = jnp.where(valid, part, 0.0).astype(BF16)


def weight_grad_kernel(counts, info, window_ref, *refs):
    out_ref = refs[-1]
    taps, rows, cells = window_ref.shape
    start = 0
    for kind, count in enumerate(counts):
        pieces = refs[start : start + count]
        start += count

        @pl.when(info[CORE] == kind)
        def _():
            slopes = jnp.concatenate([p[...].reshape(-1, p.shape[2]) for p in pieces], 0)
            for a in range(3):
                lhs = window_ref[9 * a : 9 * a + 9].reshape(9 * rows, cells)
                grad = jnp.dot(lhs, slopes, preferred_element_type=F32)
                out_ref[9 * a : 9 * a + 9] = grad.reshape(9, rows, -1)


def shards(features, section_weight, section_bias, cotangent):
    sections = lax.axis_size("section")
    spaces = lax.axis_size("space")
    half = sections // 2
    chips = sections // 2
    section = lax.axis_index("section")
    place = lax.axis_index("space")
    chip, core = section // 2, section % 2
    _, depth, row, ch = features.shape
    cells = depth * row

    weight = jnp.transpose(section_weight[0], (1, 0, 2))
    doubled = (section == 0) | (section == half)
    weight_act = weight[:, :ch]
    weight_act = jnp.where(
        doubled, (weight_act.astype(F32) + weight[:, ch:].astype(F32)).astype(BF16), weight_act
    )
    bias = section_bias.reshape(1, 1, ch)
    at = (place + jnp.arange(-1, 2)) % spaces
    info = jnp.concatenate(
        [jnp.stack([core, section]), (at > 0), (at < spaces - 1)]
    ).astype(jnp.int32)
    vmem = pl.BlockSpec(memory_space=pltpu.VMEM)
    smem = pl.BlockSpec(memory_space=pltpu.SMEM)

    def call(kernel, ins, outs, pads, side=None):
        specs = [smem] + [vmem] * (len(ins) - 1)
        scratch = [pltpu.VMEM((pads, (depth + 2) * row, ch), BF16)] if pads else []
        if side is not None:
            specs[side] = pl.BlockSpec(memory_space=pl.ANY)
            scratch += [pltpu.VMEM((27, ch, ch), BF16), pltpu.SemaphoreType.DMA((3,))]
        many = isinstance(outs, list)
        return pl.pallas_call(
            kernel,
            out_shape=[jax.ShapeDtypeStruct((n, cells, ch), t) for n, t in outs] if many else outs,
            in_specs=specs,
            out_specs=[vmem] * len(outs) if many else vmem,
            scratch_shapes=scratch,
            compiler_params=pltpu.CompilerParams(vmem_limit_bytes=48 * 2**20),
        )(*ins)

    def forward(count, k, slices, base, old):
        return call(
            functools.partial(forward_kernel, count, k, row),
            [info, *slices, weight_act, base, *old],
            [(count, BF16), (count, BF16), (1, BF16)],
            3 * count,
        )

    def wide_back(k, cots, facs, skip, fac, even, old):
        return call(
            functools.partial(wide_back_kernel, k, not old, row),
            [info, *cots, *facs, skip, fac, even, weight_act, *old],
            [(3, BF16), (5, BF16), (3, BF16)],
            9,
        )

    def narrow_back(k, got, skip, extra, fac, old):
        return call(
            functools.partial(narrow_back_kernel, k, not old, row),
            [info, got, skip, extra, fac, weight_act, *old],
            [(1, BF16), (1, F32), (3, BF16)],
            3,
        )

    def side_part(needed, *sides):
        def run(weight, bias, *sides):
            return call(
                functools.partial(side_kernel, row, len(sides) == 5),
                [info, *sides, weight, bias],
                [(3, F32)],
                9,
                1 + len(sides),
            )[0]

        def skip(weight, bias, *sides):
            return jnp.broadcast_to(bias, (3, cells, ch))

        return lax.cond(needed, run, skip, weight, bias, *sides)

    def side_back(needed, odd, even):
        def run(weight, odd, even):
            return call(
                functools.partial(side_back_kernel, row), [info, odd, even, weight], [(3, BF16)], 9, 3
            )[0]

        def skip(weight, odd, even):
            return jnp.zeros((3, cells, ch), BF16)

        return lax.cond(needed, run, skip, weight, odd, even)

    def sibling(block):
        return lax.ppermute(block, "section", [(s, s ^ 1) for s in range(sections)])

    def around(block, d):
        return lax.ppermute(block, "space", [(i, (i + d) % spaces) for i in range(spaces)])

    def across(block, d, *pairs):
        route = [
            (s * spaces + i, t * spaces + (i + d) % spaces) for s, t in pairs for i in range(spaces)
        ]
        return lax.ppermute(block, BOTH, route)

    def hop(block, *pairs):
        moved = {d: across(block, d, *pairs) for d in (2, -2, 1, -1, 0)}
        return [moved[d] for d in (2, 1, 0, -1, -2)]

    def along(block, *pairs):
        return lax.ppermute(block, "section", pairs)

    def after(value, *others):
        return lax.optimization_barrier((value, *others))[0]

    own = features.reshape(1, cells, ch)
    cot_own = cotangent.reshape(1, cells, ch)
    pair = jnp.concatenate([own, cot_own], 0)
    got = []
    for d in (2, 1):
        route = []
        for s in range(sections):
            move = d if s % 2 == 0 else -d
            route += [(s * spaces + i, s * spaces + (i + move) % spaces) for i in range(spaces)]
        got.append(lax.ppermute(pair, BOTH, route))
    other = [sibling(g) for g in got]
    act = [got[0][:1], got[1][:1], own, other[1][:1], other[0][:1]]
    cot = [other[0][1:], other[1][1:], cot_own, got[1][1:], got[0][1:]]

    base3 = side_part((section > 0) & (section < half), *act)
    fac3 = act3 = fac1 = act1 = None
    for k in range(chips):
        old = [] if k == 0 else [fac3, act3]
        out3, fac3, act3 = forward(3, k, act, bias if k in (0, half // 2) else base3, old)
        in3 = sibling(out3)
        if k == chips - 1:
            fac_even = sibling(fac3)
        old = [] if k == 0 else [fac1, act1]
        out1, fac1, act1 = forward(1, k, [in3], base3, old)
        if k == 0:
            first3 = out3
        if k == 1:
            moved3 = along(after(jnp.where(section == 0, first3, out3), out1), (0, 7), (2, 5))
            moved5 = along(after(jnp.concatenate(act, 0), out1), (2, 6))
            late = jnp.where(section == 6, moved5, jnp.pad(moved3, ((1, 1), (0, 0), (0, 0))))
            late_base3 = side_part(section > half, late)
        if k + 1 < chips:
            act = hop(out1, (1, 2), (3, 4), (5, 6))
        if k == 1:
            base3 = late_base3
    side_own = jnp.where(section < half, own, jnp.where(section == half, act3, late[2:3]))
    act_own = jnp.where(core == 0, act3, act1)

    moved = {d: around(fac1, d) for d in (2, -2, 1, -1)}
    facs = [moved[2], moved[1], fac1, moved[-1], moved[-2]]
    none = jnp.zeros((3, cells, ch), BF16)
    skip_wide, skip_narrow, extra, even3 = none, none, none[:1], none
    slope5 = slope3 = None
    for k in reversed(range(chips)):
        old = [] if slope5 is None else [slope5]
        send, slope5, even3 = wide_back(k, cot, facs, skip_wide, fac_even, even3, old)
        got = sibling(send)
        old = [] if slope3 is None else [slope3]
        sent, total, slope3 = narrow_back(k, got, skip_narrow, extra, fac3, old)
        if k:
            cot = hop(sent, (2, 1), (4, 3), (6, 5))
        if k == 2:
            back = side_back(section > half, after(slope5, sent), slope3)
            moved_7_6 = along(back, (7, 1), (6, 2))
            skip_narrow = along(back, (5, 2))
            skip_wide = jnp.where(section == 1, moved_7_6, 0)
            extra = jnp.where(section == 2, moved_7_6[1:2], 0)
            joined = after(jnp.concatenate([act_own[0], side_own[0]], 1), sent)
            blocks = jnp.transpose(joined.reshape(cells, spaces, -1), (1, 0, 2))
            blocks = lax.all_to_all(blocks, "space", 0, 0, tiled=True)
            blocks = blocks.reshape(spaces, cells, -1)
            zero = jnp.zeros_like(blocks[:1])
            lower = jnp.concatenate([zero, blocks[:-1]], 0)
            upper = jnp.concatenate([blocks[1:], zero], 0)
            shifted = jnp.stack([lower, blocks, upper])
            start = (place - 1 - core) % spaces
            shifted = lax.dynamic_slice_in_dim(
                jnp.concatenate([shifted, shifted], 1), start, spaces, axis=1
            )
            shifted = jnp.transpose(shifted.reshape(3, spaces * cells, -1), (0, 2, 1))
            window = call(
                functools.partial(lambda r, i, *refs: window_kernel(r, *refs), row),
                [info, shifted],
                jax.ShapeDtypeStruct((27, shifted.shape[1], spaces * cells), BF16),
                0,
            )
        if k == 1:
            even3 = sibling(slope3)

    down = [(q, q - 1) for q in range(1, sections, 2)]
    evens = {d: across(even3, d, *down) for d in (3, -3, 6, -6)}
    evens[8] = across(even3[1:2], 8, *down)
    odds = {d: across(slope5, d, *down) for d in (5, -5)}
    odds[8] = across(slope5[2:3], 8, *down)
    odds = {d: sibling(odds[d]) for d in odds}

    own_side = side_back(
        (section > 0) & (section < half), after(slope5, total), slope3
    )[1]
    from_next = along(own_side, (3, 1), (2, 0)).astype(F32)
    own_term = jnp.where(section == 0, total[0], own_side.astype(F32))
    term = (own_term + from_next).astype(BF16)
    width = ch // chips
    pieces = [term[:, j * width : (j + 1) * width] for j in range(chips)]
    piece = pieces[0]
    for j in (2, 1, 3):
        moved = along(pieces[j], (0, 2 * j), (1, 2 * j + 1))
        piece = jnp.where(chip == j, moved, piece)
    lower, upper = piece[:, : width // 2], piece[:, width // 2 :]
    moved = sibling(jnp.where(core == 0, upper, lower))
    grad_features = jnp.where(core == 0, lower, upper).astype(F32) + moved.astype(F32)

    even_pieces = [slope3, evens[-3], evens[-6], evens[8], evens[6], evens[3]]
    odd_pieces = [slope5, odds[-5], odds[8], odds[5]]
    grad_weight = call(
        functools.partial(weight_grad_kernel, [len(even_pieces), len(odd_pieces)]),
        [info, window, *even_pieces, *odd_pieces],
        jax.ShapeDtypeStruct((27, window.shape[1], ch), F32),
        0,
    )
    return (
        grad_features.reshape(1, depth, row, -1),
        jnp.transpose(grad_weight, (1, 0, 2))[None],
    )


def solution(mesh):
    return jax.shard_map(
        shards,
        mesh=mesh,
        in_specs=(
            P("space", None, None, None),
            P("section", None, None, None),
            P("section", None),
            P("space", None, None, None),
        ),
        out_specs=(P("space", None, None, "section"), P("section", "space", None, None)),
        check_vma=False,
    )
```

```python
import functools

import jax
import jax.numpy as jnp
from jax import lax
from jax.experimental import pallas as pl
from jax.experimental.pallas import tpu as pltpu
from jax.sharding import PartitionSpec as P

BF16 = jnp.bfloat16
F32 = jnp.float32
TAPS = [(a, b) for a in range(3) for b in range(3)]
BOTH = ("section", "space")
CORE, SECTION, LOW, HIGH = 0, 1, 2, 5


def fill(pad, info, slices, count, row):
    zero = jnp.zeros((pad.shape[0], row, pad.shape[2]), BF16)
    pad[:, :row, :] = zero
    pad[:, pad.shape[1] - row :, :] = zero
    first = 1 if count == 1 else 0
    for j in range(count):
        low = info[LOW + first + j] > 0
        high = info[HIGH + first + j] > 0
        values = [
            jnp.where(low, slices[j], jnp.zeros_like(slices[j])),
            slices[j + 1],
            jnp.where(high, slices[j + 2], jnp.zeros_like(slices[j])),
        ]
        for a in range(3):
            pad[a * count + j, row : pad.shape[1] - row, :] = values[a]


def shift_sum(low, mid, high, row):
    rows = mid.shape[0]
    y = lax.broadcasted_iota(jnp.int32, mid.shape, 0) % row
    low = jnp.where(y == 0, 0.0, pltpu.roll(low, 1, 0))
    high = jnp.where(y == row - 1, 0.0, pltpu.roll(high, rows - 1, 0))
    return mid + low + high


def taps_of(pad, first, w_ref, c, taps, count, row, flip):
    ch = pad.shape[2]
    cells = pad.shape[1] - 2 * row
    total = None
    for a, b in taps:
        lhs = pad[pl.ds(first + a * count, count), b * row : b * row + cells, :]
        tap = 9 * a + 3 * b + c
        if flip:
            tap = w_ref.shape[0] - 1 - tap
        part = lax.dot_general(
            lhs.reshape(count * cells, ch),
            w_ref[tap],
            (((1,), (1 if flip else 0,)), ((), ())),
            preferred_element_type=F32,
        )
        total = part if total is None else total + part
    return total


def conv(pad, w_ref, count, row, flip):
    parts = [taps_of(pad, 0, w_ref, c, TAPS, count, row, flip) for c in range(3)]
    return shift_sum(*parts, row).reshape(count, -1, pad.shape[2])


def pack_kernel(*refs):
    for i, ref in enumerate(refs[:-1]):
        refs[-1][i : i + 1] = ref[...]


def forward_kernel(count, k, row, info, *refs):
    cut = 5 if count == 3 else 1
    slices, refs = refs[:cut], refs[cut:]
    w_ref, base_ref, refs = refs[0], refs[1], refs[2:]
    wide = count == 3 and k == 1
    if wide:
        first_ref, refs = refs[0], refs[1:]
    out_ref, keep_ref, refs = refs[0], refs[1], refs[2:]
    if wide:
        all_ref, refs = refs[0], refs[1:]
    pad = refs[0]
    own = info[SECTION] == 2 * k + (0 if count == 3 else 1)

    @pl.when(own)
    def _():
        values = [s[0] for s in slices] if count == 3 else [slices[0][i] for i in range(3)]
        fill(pad, info, values, count, row)
        base = base_ref[...]
        if count == 1 and base.shape[0] == 3:
            base = base[1:2]
        preact = conv(pad, w_ref, count, row, False) + base
        logistic = jax.nn.sigmoid(preact)
        act = jnp.stack(values[1 : 1 + count]).astype(F32)
        out_ref[...] = (act + preact * logistic).astype(BF16)
        keep_ref[:count] = (logistic * (1.0 + preact * (1.0 - logistic))).astype(BF16)
        keep_ref[count] = values[2] if count == 3 else values[1]

    @pl.when(jnp.logical_not(own))
    def _():
        keep_ref[...] = jnp.zeros_like(keep_ref)
        out_ref[...] = first_ref[...] if wide else jnp.zeros_like(out_ref)

    if wide:
        for i in range(5):
            all_ref[i] = slices[i][0]


def wide_back_kernel(k, chips, row, info, *refs):
    cots, refs = refs[:5], refs[5:]
    w_ref, refs = refs[0], refs[1:]
    if k == chips - 1:
        facs, refs = refs[:6], refs[6:]
    else:
        facs_ref, refs = refs[0], refs[1:]
    if k == 0:
        skip_ref, even_old, slope_old, refs = refs[0], refs[1], refs[2], refs[3:]
    send_ref, slope_ref, extra_ref, pad = refs
    own = info[SECTION] == 2 * k + 1
    if k == chips - 1:
        for i in range(5):
            extra_ref[i] = facs[i][0]
        extra_ref[5:] = facs[5][:3]

    @pl.when(own)
    def _():
        cot = [c[c.shape[0] - 1].astype(F32) for c in cots]
        fac = [f[0] for f in facs[:5]] if k == chips - 1 else [facs_ref[i] for i in range(5)]
        slope = [(c * f.astype(F32)).astype(BF16) for c, f in zip(cot, fac)]
        for i in range(5):
            slope_ref[i] = slope[i]
        fill(pad, info, slope, 3, row)
        sent = (jnp.stack(cot[1:4]) + conv(pad, w_ref, 3, row, True)).astype(BF16)
        if k == 0:
            sent = (sent.astype(F32) + skip_ref[...].astype(F32)).astype(BF16)
            even = (sent.astype(F32) * facs_ref[5:].astype(F32)).astype(BF16)
            extra_ref[:3] = even
            extra_ref[3] = even[1]
            extra_ref[4] = slope[2]
        send_ref[...] = sent

    @pl.when(jnp.logical_not(own))
    def _():
        send_ref[...] = jnp.zeros_like(send_ref)
        if k == 0:
            slope_ref[...] = slope_old[...]
            extra_ref[:3] = even_old[...]
            extra_ref[3] = even_old[1]
            extra_ref[4] = slope_old[2]
        else:
            slope_ref[...] = jnp.zeros_like(slope_ref)


def narrow_back_kernel(k, row, info, *refs):
    got_ref, keep_ref, w_ref, refs = refs[0], refs[1], refs[2], refs[3:]
    if k == 1:
        skip_ref, next_ref, refs = refs[0], refs[1], refs[2:]
    if k == 0:
        (slope_old, odd_ref, w_hbm), refs = refs[:3], refs[3:]
    sent_ref, slope_ref, refs = refs[0], refs[1], refs[2:]
    if k == 0:
        pad, w_side, pad_side, sem = refs
    else:
        pad = refs[0]

    @pl.when(info[SECTION] == 2 * k)
    def _():
        cot = got_ref[...]
        if k == 1:
            cot = (cot.astype(F32) + skip_ref[...].astype(F32)).astype(BF16)
        slope = (cot.astype(F32) * keep_ref[:3].astype(F32)).astype(BF16)
        slope_ref[...] = slope
        fill(pad, info, [slope[i] for i in range(3)], 1, row)
        total = cot[1:2].astype(F32) + conv(pad, w_ref, 1, row, True)
        if k == 1:
            total = total + next_ref[1:2].astype(F32)
        sent_ref[...] = total.astype(sent_ref.dtype)

    @pl.when(info[SECTION] != 2 * k)
    def _():
        slope_ref[...] = slope_old[...] if k == 0 else jnp.zeros_like(slope_ref)
        if k == 0:

            @pl.when(info[SECTION] == 1)
            def _():
                ch = pad.shape[2]
                copy = pltpu.make_async_copy(w_hbm.at[:, pl.ds(ch, ch)], w_side, sem)
                copy.start()
                fill(pad_side, info, [odd_ref[i] for i in range(1, 4)], 1, row)
                copy.wait()
                sent_ref[...] = conv(pad_side, w_side, 1, row, True)

            @pl.when(info[SECTION] > 1)
            def _():
                sent_ref[...] = jnp.zeros_like(sent_ref)

        else:
            sent_ref[...] = jnp.zeros_like(sent_ref)


def side_conv(values, flip, row, info, w_hbm, pad, w_ref, sems):
    ch = pad.shape[2]
    copies = []
    for i in range(3):
        taps = pl.ds(9 * i, 9)
        copy = pltpu.make_async_copy(w_hbm.at[taps, pl.ds(ch, ch)], w_ref.at[taps], sems.at[i])
        copies.append(copy)
    for i in (2, 1, 0) if flip else (0, 1, 2):
        copies[i].start()
    fill(pad, info, values, 3, row)
    parts = [None] * 3
    for a in range(3):
        copies[2 - a if flip else a].wait()
        for c in range(3):
            taps = [(a, b) for b in range(3)]
            part = taps_of(pad, 0, w_ref, c, taps, 3, row, flip)
            parts[c] = part if parts[c] is None else parts[c] + part
    return shift_sum(*parts, row).reshape(3, -1, ch)


def side_kernel(row, early, info, *refs):
    count = 5 if early else 1
    sides, (w_hbm, bias_ref, out_ref, pad, w_ref, sems) = refs[:count], refs[count:]
    if early:
        got = [s[0] for s in sides]
        values = [jnp.where(info[CORE] == 0, got[i], got[4 - i]) for i in range(5)]
    else:
        values = [sides[0][i] for i in range(5)]
    out_ref[...] = side_conv(values, False, row, info, w_hbm, pad, w_ref, sems) + bias_ref[...]


def side_back_kernel(row, info, odd_ref, even_ref, w_hbm, out_ref, pad, w_ref, sems):
    zero = jnp.zeros_like(even_ref[0])
    even = [zero, even_ref[0], even_ref[1], even_ref[2], zero]
    values = [jnp.where(info[CORE] == 1, odd_ref[i], even[i]) for i in range(5)]
    out_ref[...] = side_conv(values, True, row, info, w_hbm, pad, w_ref, sems).astype(BF16)


def window_kernel(row, joined_ref, out_ref):
    cells = joined_ref.shape[2]
    cell = lax.broadcasted_iota(jnp.int32, joined_ref.shape[1:], 1)
    z = cell // row % 4
    y = cell % row
    for a in range(3):
        value = joined_ref[a].astype(F32)
        for b, c in TAPS:
            move = (b - 1) * row + (c - 1)
            part = value if move == 0 else pltpu.roll(value, (-move) % cells, 1)
            valid = (z + b - 1 >= 0) & (z + b - 1 < 4) & (y + c - 1 >= 0) & (y + c - 1 < row)
            out_ref[9 * a + 3 * b + c] = jnp.where(valid, part, 0.0).astype(BF16)


def weight_grad_kernel(counts, info, window_ref, *refs):
    out_ref = refs[-1]
    taps, rows, cells = window_ref.shape
    start = 0
    for kind, count in enumerate(counts):
        pieces = refs[start : start + count]
        start += count

        @pl.when(info[CORE] == kind)
        def _():
            parts = [p[kind : kind + 1] if p.shape[0] == 2 else p[...] for p in pieces]
            slopes = jnp.concatenate([p.reshape(-1, p.shape[2]) for p in parts], 0)
            for a in range(3):
                lhs = window_ref[9 * a : 9 * a + 9].reshape(9 * rows, cells)
                grad = jnp.dot(lhs, slopes, preferred_element_type=F32)
                out_ref[9 * a : 9 * a + 9] = grad.reshape(9, rows, -1)


def shards(features, section_weight, section_bias, cotangent):
    sections = lax.axis_size("section")
    spaces = lax.axis_size("space")
    half = sections // 2
    chips = sections // 2
    section = lax.axis_index("section")
    place = lax.axis_index("space")
    chip, core = section // 2, section % 2
    _, depth, row, ch = features.shape
    cells = depth * row

    weight = jnp.transpose(section_weight[0], (1, 0, 2))
    doubled = (section == 0) | (section == half)
    weight_act = weight[:, :ch]
    weight_act = jnp.where(
        doubled, (weight_act.astype(F32) + weight[:, ch:].astype(F32)).astype(BF16), weight_act
    )
    bias = section_bias.reshape(1, 1, ch)
    at = (place + jnp.arange(-1, 2)) % spaces
    info = jnp.concatenate(
        [jnp.stack([core, section]), (at > 0), (at < spaces - 1)]
    ).astype(jnp.int32)
    vmem = pl.BlockSpec(memory_space=pltpu.VMEM)
    smem = pl.BlockSpec(memory_space=pltpu.SMEM)

    def call(kernel, ins, outs, pads, side=None):
        specs = [vmem if i or kernel is pack_kernel else smem for i in range(len(ins))]
        scratch = [pltpu.VMEM((pads, (depth + 2) * row, ch), BF16)] if pads else []
        if side is not None:
            specs[side] = pl.BlockSpec(memory_space=pl.ANY)
            scratch.append(pltpu.VMEM((27, ch, ch), BF16))
            if pads == 3:
                scratch += [pltpu.VMEM((3, (depth + 2) * row, ch), BF16), pltpu.SemaphoreType.DMA]
            else:
                scratch.append(pltpu.SemaphoreType.DMA((3,)))
        many = isinstance(outs, list)
        return pl.pallas_call(
            kernel,
            out_shape=[jax.ShapeDtypeStruct((n, cells, ch), t) for n, t in outs] if many else outs,
            in_specs=specs,
            out_specs=[vmem] * len(outs) if many else vmem,
            scratch_shapes=scratch,
            compiler_params=pltpu.CompilerParams(vmem_limit_bytes=16 * 2**20),
        )(*ins)

    def forward(count, k, slices, base, first=()):
        return call(
            functools.partial(forward_kernel, count, k, row),
            [info, *slices, weight_act, base, *first],
            [(count, BF16), (count + 1, BF16)] + [(5, BF16) for _ in first],
            3 * count,
        )

    def wide_back(k, cots, facs, *more):
        last = 8 if k == chips - 1 else 5
        return call(
            functools.partial(wide_back_kernel, k, chips, row),
            [info, *cots, weight_act, *facs, *more],
            [(3, BF16), (5, BF16), (last, BF16)],
            9,
        )

    def narrow_back(k, got, keep, *more):
        return call(
            functools.partial(narrow_back_kernel, k, row),
            [info, got, keep, weight_act, *more],
            [(1, F32 if k == 0 else BF16), (3, BF16)],
            3,
            6 if k == 0 else None,
        )

    def side_part(needed, *sides):
        def run(weight, bias, *sides):
            return call(
                functools.partial(side_kernel, row, len(sides) == 5),
                [info, *sides, weight, bias],
                [(3, F32)],
                9,
                1 + len(sides),
            )[0]

        def skip(weight, bias, *sides):
            return jnp.broadcast_to(bias, (3, cells, ch))

        return lax.cond(needed, run, skip, weight, bias, *sides)

    def side_back(needed, odd, even):
        def run(weight, odd, even):
            return call(
                functools.partial(side_back_kernel, row), [info, odd, even, weight], [(3, BF16)], 9, 3
            )[0]

        def skip(weight, odd, even):
            return jnp.zeros((3, cells, ch), BF16)

        return lax.cond(needed, run, skip, weight, odd, even)

    def sibling(block):
        return lax.ppermute(block, "section", [(s, s ^ 1) for s in range(sections)])

    def around(block, d):
        return lax.ppermute(block, "space", [(i, (i + d) % spaces) for i in range(spaces)])

    def across(block, d, *pairs):
        route = [
            (s * spaces + i, t * spaces + (i + d) % spaces) for s, t in pairs for i in range(spaces)
        ]
        return lax.ppermute(block, BOTH, route)

    def hop(block, *pairs):
        moved = {d: across(block, d, *pairs) for d in (2, -2, 1, -1, 0)}
        return [moved[d] for d in (2, 1, 0, -1, -2)]

    def along(block, *pairs):
        return lax.ppermute(block, "section", pairs)

    def after(value, *others):
        return lax.optimization_barrier((value, *others))[0]

    own = features.reshape(1, cells, ch)
    cot_own = cotangent.reshape(1, cells, ch)
    pair = call(pack_kernel, [own, cot_own], [(2, BF16)], 0)[0]
    got = []
    for d in (2, 1):
        route = []
        for s in range(sections):
            move = d if s % 2 == 0 else -d
            route += [(s * spaces + i, s * spaces + (i + move) % spaces) for i in range(spaces)]
        got.append(lax.ppermute(pair, BOTH, route))
    other = [sibling(g) for g in got]
    act = [got[0], got[1], own, other[1], other[0]]
    cot = [other[0], other[1], cot_own, got[1], got[0]]

    base3 = side_part((section > 0) & (section < half), *act)
    act = list(after(tuple(act), base3))
    keeps3, keeps1 = [], []
    for k in range(chips):
        base = bias if k in (0, half // 2) else base3
        if k == 1:
            out3, keep3, act5 = forward(3, k, act, base, [first3])
        else:
            out3, keep3 = forward(3, k, act, base)
        in3 = sibling(out3)
        keeps3.append(keep3)
        if k == chips - 1:
            keep3 = sum(keeps3[1:], keeps3[0])
            fac_even = sibling(keep3)
        out1, keep1 = forward(1, k, [in3], base3)
        keeps1.append(keep1)
        if k == 0:
            first3 = out3
        if k + 1 < chips:
            act = hop(out1, (1, 2), (3, 4), (5, 6))
        if k == 1:
            moved3 = along(after(out3, out1), (0, 7), (2, 5))
            moved5 = along(after(act5, out1), (2, 6))
            late = jnp.where(section == 6, moved5, jnp.pad(moved3, ((1, 1), (0, 0), (0, 0))))
            base3 = side_part(section > half, late)
            act = list(after(tuple(act), base3))
    keep1 = sum(keeps1[1:], keeps1[0])

    fac1 = keep1[:1]
    moved = {d: around(fac1, d) for d in (2, -2, 1, -1)}
    facs = [moved[2], moved[1], fac1, moved[-1], moved[-2], fac_even]
    act_own = jnp.where(core == 0, keep3[3:], keep1[1:])
    side_own = jnp.where(section < half, own, jnp.where(section == half, act_own, late[2:3]))

    def exchange(needed, act, side):
        def run(act, side):
            joined = jnp.concatenate([act[0], side[0]], 1)
            blocks = jnp.transpose(joined.reshape(cells, spaces, -1), (1, 0, 2))
            return lax.all_to_all(blocks, "space", 0, 0, tiled=True).reshape(spaces, cells, -1)

        def skip(act, side):
            return jnp.zeros((spaces, cells, 2 * ch // spaces), BF16)

        return lax.cond(needed, run, skip, act, side)

    slopes5, slopes3 = [], []
    for k in reversed(range(chips)):
        more = []
        if k == 0:
            more = [moved_7_6, even3, sum(slopes5[1:], slopes5[0])]
        send, slope5, extra = wide_back(k, cot, facs if k == chips - 1 else [facs], *more)
        if k == chips - 1:
            facs = extra
        got = sibling(send)
        if k == 0:
            down = [(q, q - 1) for q in range(1, sections, 2)]
            evens = {d: across(extra[:3], d, *down) for d in (3, -3, 6, -6)}
            odds = {d: across(slope5, d, *down) for d in (5, -5)}
            opposite = across(extra[3:], 8, *down)
            got, evens, odds, opposite = lax.optimization_barrier((got, evens, odds, opposite))
            back = side_back((section == 2) | (section == 3), after(old5, send), old3)
            from_next = along(back[1], (3, 1), (2, 0))
            sent, slope3 = narrow_back(k, got, keep3, old3, slope5, weight)
            continue
        more = [skip_narrow, moved_7_6] if k == 1 else []
        sent, slope3 = narrow_back(k, got, keep3, *more)
        slopes5.append(slope5)
        slopes3.append(slope3)
        cot = hop(sent, (2, 1), (4, 3), (6, 5))
        if k == 2:
            back = side_back(
                section > half,
                after(slopes5[0] + slopes5[1], sent),
                slopes3[0] + slopes3[1],
            )
            moved_7_6 = along(back, (7, 1), (6, 2))
            skip_narrow = along(back, (5, 2))
            late_blocks = exchange(
                section >= half, *after((act_own, side_own), moved_7_6, skip_narrow)
            )
            cot, moved_7_6, skip_narrow, late_blocks = lax.optimization_barrier(
                (cot, moved_7_6, skip_narrow, late_blocks)
            )
        if k == 3:
            blocks = exchange(section < half, *after((act_own, side_own), send))
            cot, blocks = lax.optimization_barrier((cot, blocks))
        if k == 1:
            old5 = sum(slopes5[1:], slopes5[0])
            old3 = sum(slopes3[1:], slopes3[0])
            even3 = sibling(old3)
            blocks = blocks + late_blocks
            zero = jnp.zeros_like(blocks[:1])
            lower = jnp.concatenate([zero, blocks[:-1]], 0)
            upper = jnp.concatenate([blocks[1:], zero], 0)
            shifted = jnp.stack([lower, blocks, upper])
            start = (place - 1 - core) % spaces
            shifted = lax.dynamic_slice_in_dim(
                jnp.concatenate([shifted, shifted], 1), start, spaces, axis=1
            )
            shifted = jnp.transpose(shifted.reshape(3, spaces * cells, -1), (0, 2, 1))
            window = call(
                functools.partial(lambda r, i, *refs: window_kernel(r, *refs), row),
                [info, shifted],
                jax.ShapeDtypeStruct((27, shifted.shape[1], spaces * cells), BF16),
                0,
            )
            old5, old3, even3, window = lax.optimization_barrier((old5, old3, even3, window))

    odds = {d: sibling(odds[d]) for d in odds}
    back_opposite = sibling(opposite)

    term = (sent[0] + from_next.astype(F32)).astype(BF16)
    width = ch // chips
    pieces = [term[:, j * width : (j + 1) * width] for j in range(chips)]
    piece = pieces[0]
    for j in (2, 1, 3):
        moved = along(pieces[j], (0, 2 * j), (1, 2 * j + 1))
        piece = jnp.where(chip == j, moved, piece)
    lower, upper = piece[:, : width // 2], piece[:, width // 2 :]
    moved = sibling(jnp.where(core == 0, upper, lower))
    grad_features = jnp.where(core == 0, lower, upper).astype(F32) + moved.astype(F32)

    even_pieces = [slope3, evens[-3], evens[-6], opposite, evens[6], evens[3]]
    odd_pieces = [slope5, odds[-5], back_opposite, odds[5]]
    grad_weight = call(
        functools.partial(weight_grad_kernel, [len(even_pieces), len(odd_pieces)]),
        [info, window, *even_pieces, *odd_pieces],
        jax.ShapeDtypeStruct((27, window.shape[1], ch), F32),
        0,
    )
    return (
        grad_features.reshape(1, depth, row, -1),
        jnp.transpose(grad_weight, (1, 0, 2))[None],
    )


def solution(mesh):
    return jax.shard_map(
        shards,
        mesh=mesh,
        in_specs=(
            P("space", None, None, None),
            P("section", None, None, None),
            P("section", None),
            P("space", None, None, None),
        ),
        out_specs=(P("space", None, None, "section"), P("section", "space", None, None)),
        check_vma=False,
    )
```

```python
import functools

import jax
import jax.numpy as jnp
from jax import lax
from jax.experimental import pallas as pl
from jax.experimental.pallas import tpu as pltpu
from jax.sharding import PartitionSpec as P

BF16 = jnp.bfloat16
F32 = jnp.float32
TAPS = [(a, b) for a in range(3) for b in range(3)]
BOTH = ("section", "space")
CORE, SECTION, LOW, HIGH = 0, 1, 2, 5


def fill(pad, info, slices, count, row):
    zero = jnp.zeros((pad.shape[0], row, pad.shape[2]), BF16)
    pad[:, :row, :] = zero
    pad[:, pad.shape[1] - row :, :] = zero
    first = 1 if count == 1 else 0
    for j in range(count):
        low = info[LOW + first + j] > 0
        high = info[HIGH + first + j] > 0
        values = [
            jnp.where(low, slices[j], jnp.zeros_like(slices[j])),
            slices[j + 1],
            jnp.where(high, slices[j + 2], jnp.zeros_like(slices[j])),
        ]
        for a in range(3):
            pad[a * count + j, row : pad.shape[1] - row, :] = values[a]


def shift_sum(low, mid, high, row):
    rows = mid.shape[0]
    y = lax.broadcasted_iota(jnp.int32, mid.shape, 0) % row
    low = jnp.where(y == 0, 0.0, pltpu.roll(low, 1, 0))
    high = jnp.where(y == row - 1, 0.0, pltpu.roll(high, rows - 1, 0))
    return mid + low + high


def taps_of(pad, first, w_ref, c, taps, count, row, flip):
    ch = pad.shape[2]
    cells = pad.shape[1] - 2 * row
    total = None
    for a, b in taps:
        lhs = pad[pl.ds(first + a * count, count), b * row : b * row + cells, :]
        tap = 9 * a + 3 * b + c
        if flip:
            tap = w_ref.shape[0] - 1 - tap
        part = lax.dot_general(
            lhs.reshape(count * cells, ch),
            w_ref[tap],
            (((1,), (1 if flip else 0,)), ((), ())),
            preferred_element_type=F32,
        )
        total = part if total is None else total + part
    return total


def conv(pad, w_ref, count, row, flip):
    parts = [taps_of(pad, 0, w_ref, c, TAPS, count, row, flip) for c in range(3)]
    return shift_sum(*parts, row).reshape(count, -1, pad.shape[2])


def conv_loop(pad, w_ref, count, row, flip):
    ch = pad.shape[2]
    cells = pad.shape[1] - 2 * row

    def step(a, parts):
        new = list(parts)
        for b in range(3):
            lhs = pad[pl.ds(a * count, count), b * row : b * row + cells, :]
            lhs = lhs.reshape(count * cells, ch)
            for c in range(3):
                tap = 9 * a + 3 * b + c
                if flip:
                    tap = 26 - tap
                new[c] = new[c] + lax.dot_general(
                    lhs,
                    w_ref[tap],
                    (((1,), (1 if flip else 0,)), ((), ())),
                    preferred_element_type=F32,
                )
        return tuple(new)

    zero = jnp.zeros((count * cells, ch), F32)
    parts = lax.fori_loop(0, 3, step, (zero, zero, zero))
    return shift_sum(*parts, row).reshape(count, cells, ch)


def pack_kernel(*refs):
    for i, ref in enumerate(refs[:-1]):
        refs[-1][i : i + 1] = ref[...]


def forward_kernel(count, k, row, info, *refs):
    cut = 5 if count == 3 else 1
    slices, refs = refs[:cut], refs[cut:]
    w_ref, base_ref, refs = refs[0], refs[1], refs[2:]
    wide = count == 3 and k == 1
    if wide:
        first_ref, refs = refs[0], refs[1:]
    out_ref, keep_ref, refs = refs[0], refs[1], refs[2:]
    if wide:
        all_ref, refs = refs[0], refs[1:]
    pad = refs[0]
    own = info[SECTION] == 2 * k + (0 if count == 3 else 1)

    @pl.when(own)
    def _():
        values = [s[0] for s in slices] if count == 3 else [slices[0][i] for i in range(3)]
        fill(pad, info, values, count, row)
        base = base_ref[...]
        if count == 1 and base.shape[0] == 3:
            base = base[1:2]
        preact = conv(pad, w_ref, count, row, False) + base
        logistic = jax.nn.sigmoid(preact)
        act = jnp.stack(values[1 : 1 + count]).astype(F32)
        out_ref[...] = (act + preact * logistic).astype(BF16)
        keep_ref[:count] = (logistic * (1.0 + preact * (1.0 - logistic))).astype(BF16)
        keep_ref[count] = values[2] if count == 3 else values[1]

    @pl.when(jnp.logical_not(own))
    def _():
        keep_ref[...] = jnp.zeros_like(keep_ref)
        out_ref[...] = first_ref[...] if wide else jnp.zeros_like(out_ref)

    if wide:
        for i in range(5):
            all_ref[i] = slices[i][0]


def wide_back_kernel(k, chips, row, info, *refs):
    cots, refs = refs[:5], refs[5:]
    w_ref, refs = refs[0], refs[1:]
    if k == chips - 1:
        facs, refs = refs[:6], refs[6:]
    else:
        facs_ref, refs = refs[0], refs[1:]
    if k == 0:
        skip_ref, even_old, slope_old, refs = refs[0], refs[1], refs[2], refs[3:]
    send_ref, slope_ref, refs = refs[0], refs[1], refs[2:]
    if k == chips - 1:
        extra_ref, refs = refs[0], refs[1:]
    if k == 0:
        even_ref, pair_ref, refs = refs[0], refs[1], refs[2:]
    pad = refs[0]
    own = info[SECTION] == 2 * k + 1
    if k == chips - 1:
        for i in range(5):
            extra_ref[i] = facs[i][0]
        extra_ref[5:] = facs[5][:3]

    @pl.when(own)
    def _():
        cot = [c[c.shape[0] - 1].astype(F32) for c in cots]
        fac = [f[0] for f in facs[:5]] if k == chips - 1 else [facs_ref[i] for i in range(5)]
        slope = [(c * f.astype(F32)).astype(BF16) for c, f in zip(cot, fac)]
        for i in range(5):
            slope_ref[i] = slope[i]
        fill(pad, info, slope, 3, row)
        sent = (jnp.stack(cot[1:4]) + conv(pad, w_ref, 3, row, True)).astype(BF16)
        if k == 0:
            sent = (sent.astype(F32) + skip_ref[...].astype(F32)).astype(BF16)
            even = (sent.astype(F32) * facs_ref[5:].astype(F32)).astype(BF16)
            even_ref[:3] = even
            for i in range(3):
                even_ref[3 + i] = slope[1 + i]
            pair_ref[0] = even[1]
            pair_ref[1] = slope[2]
        send_ref[...] = sent

    @pl.when(jnp.logical_not(own))
    def _():
        send_ref[...] = jnp.zeros_like(send_ref)
        if k == 0:
            slope_ref[...] = slope_old[...]
            even_ref[:3] = even_old[...]
            even_ref[3:] = slope_old[1:4]
            pair_ref[0] = even_old[1]
            pair_ref[1] = slope_old[2]
        else:
            slope_ref[...] = jnp.zeros_like(slope_ref)


def narrow_back_kernel(k, row, info, *refs):
    got_ref, keep_ref, w_ref, refs = refs[0], refs[1], refs[2], refs[3:]
    if k == 1:
        skip_ref, next_ref, refs = refs[0], refs[1], refs[2:]
    if k == 0:
        (slope_old, odd_ref, w_hbm), refs = refs[:3], refs[3:]
    sent_ref, slope_ref, refs = refs[0], refs[1], refs[2:]
    if k == 0:
        pad, w_side, pad_side, sems = refs
    else:
        pad = refs[0]

    @pl.when(info[SECTION] == 2 * k)
    def _():
        cot = got_ref[...]
        if k == 1:
            cot = (cot.astype(F32) + skip_ref[...].astype(F32)).astype(BF16)
        slope = (cot.astype(F32) * keep_ref[:3].astype(F32)).astype(BF16)
        slope_ref[...] = slope
        fill(pad, info, [slope[i] for i in range(3)], 1, row)
        total = cot[1:2].astype(F32) + conv(pad, w_ref, 1, row, True)
        if k == 1:
            total = total + next_ref[1:2].astype(F32)
        sent_ref[...] = total.astype(sent_ref.dtype)

    @pl.when(info[SECTION] != 2 * k)
    def _():
        slope_ref[...] = slope_old[...] if k == 0 else jnp.zeros_like(slope_ref)
        if k == 0:

            @pl.when(info[SECTION] == 1)
            def _():
                values = [odd_ref[i] for i in range(1, 4)]
                sent_ref[...] = side_conv(values, True, row, info, w_hbm, pad_side, w_side, sems, 1)

            @pl.when(info[SECTION] > 1)
            def _():
                sent_ref[...] = jnp.zeros_like(sent_ref)

        else:
            sent_ref[...] = jnp.zeros_like(sent_ref)


def side_conv(values, flip, row, info, w_hbm, pad, w_ref, sems, count=3):
    ch = pad.shape[2]
    copies = []
    for i in range(3):
        taps = pl.ds(9 * i, 9)
        copy = pltpu.make_async_copy(w_hbm.at[taps, pl.ds(ch, ch)], w_ref.at[taps], sems.at[i])
        copies.append(copy)
    for copy in copies:
        copy.start()
    fill(pad, info, values, count, row)
    for copy in copies:
        copy.wait()
    return conv_loop(pad, w_ref, count, row, flip)


def side_kernel(row, early, info, *refs):
    count = 5 if early else 2
    sides, (w_hbm, bias_ref, out_ref, pad, w_ref, sems) = refs[:count], refs[count:]
    if early:
        got = [s[0] for s in sides]
        values = [jnp.where(info[CORE] == 0, got[i], got[4 - i]) for i in range(5)]
    else:
        five, three = sides
        zero = jnp.zeros_like(five[0])
        rest = [zero, three[0], three[1], three[2], zero]
        values = [jnp.where(info[CORE] == 0, five[i], rest[i]) for i in range(5)]
    out_ref[...] = side_conv(values, False, row, info, w_hbm, pad, w_ref, sems) + bias_ref[...]


def side_back_kernel(row, info, odd_ref, even_ref, w_hbm, out_ref, pad, w_ref, sems):
    zero = jnp.zeros_like(even_ref[0])
    even = [zero, even_ref[0], even_ref[1], even_ref[2], zero]
    values = [jnp.where(info[CORE] == 1, odd_ref[i], even[i]) for i in range(5)]
    out_ref[...] = side_conv(values, True, row, info, w_hbm, pad, w_ref, sems).astype(BF16)


def window_kernel(row, joined_ref, out_ref):
    cells = joined_ref.shape[2]
    cell = lax.broadcasted_iota(jnp.int32, joined_ref.shape[1:], 1)
    z = cell // row % 4
    y = cell % row
    for a in range(3):
        value = joined_ref[a].astype(F32)
        for b, c in TAPS:
            move = (b - 1) * row + (c - 1)
            part = value if move == 0 else pltpu.roll(value, (-move) % cells, 1)
            valid = (z + b - 1 >= 0) & (z + b - 1 < 4) & (y + c - 1 >= 0) & (y + c - 1 < row)
            out_ref[9 * a + 3 * b + c] = jnp.where(valid, part, 0.0).astype(BF16)


def weight_grad_kernel(counts, info, window_hbm, *refs):
    out_ref, window_ref, slopes_ref, sems = refs[-4:]
    taps, rows, cells = window_ref.shape
    ch = slopes_ref.shape[2]
    lanes = [
        pltpu.make_async_copy(window_hbm.at[pl.ds(9 * a, 9)], window_ref.at[pl.ds(9 * a, 9)], sems.at[a])
        for a in range(3)
    ]
    for copy in lanes:
        copy.start()
    start = 0
    for kind, count in enumerate(counts):
        pieces = refs[start : start + count]
        start += count

        @pl.when(info[CORE] == kind)
        def _():
            copies, place = [], 0
            for i, piece in enumerate(pieces):
                size = 1 if piece.shape[0] == 2 else 3
                first = {2: kind, 3: 0, 5: 1, 6: 3 * kind}[piece.shape[0]]
                source = piece.at[pl.ds(first, size)]
                target = slopes_ref.at[pl.ds(place, size)]
                copies.append(pltpu.make_async_copy(source, target, sems.at[3 + i]))
                place += size
            for copy in copies:
                copy.start()
            for copy in copies:
                copy.wait()

    slopes = slopes_ref[...].reshape(cells, ch)
    for a in range(3):
        lanes[a].wait()
        lhs = window_ref[9 * a : 9 * a + 9].reshape(9 * rows, cells)
        grad = jnp.dot(lhs, slopes, preferred_element_type=F32)
        out_ref[9 * a : 9 * a + 9] = grad.reshape(9, rows, -1)


def shards(features, section_weight, section_bias, cotangent):
    sections = lax.axis_size("section")
    spaces = lax.axis_size("space")
    half = sections // 2
    chips = sections // 2
    section = lax.axis_index("section")
    place = lax.axis_index("space")
    chip, core = section // 2, section % 2
    _, depth, row, ch = features.shape
    cells = depth * row

    weight = jnp.transpose(section_weight[0], (1, 0, 2))
    doubled = (section == 0) | (section == half)
    weight_act = weight[:, :ch]
    weight_act = jnp.where(
        doubled, (weight_act.astype(F32) + weight[:, ch:].astype(F32)).astype(BF16), weight_act
    )
    bias = section_bias.reshape(1, 1, ch)
    at = (place + jnp.arange(-1, 2)) % spaces
    info = jnp.concatenate(
        [jnp.stack([core, section]), (at > 0), (at < spaces - 1)]
    ).astype(jnp.int32)
    vmem = pl.BlockSpec(memory_space=pltpu.VMEM)
    smem = pl.BlockSpec(memory_space=pltpu.SMEM)

    def far(value):
        return pltpu.with_memory_space_constraint(value, pltpu.HBM)

    def call(kernel, ins, outs, pads, side=None, deps=(), pin=False):
        count, kept = len(ins), len(ins) + len(deps)
        specs = [vmem if i or kernel is pack_kernel else smem for i in range(count)]
        specs += [pl.BlockSpec(memory_space=pltpu.HBM)] * len(deps)
        scratch = [pltpu.VMEM((pads, (depth + 2) * row, ch), BF16)] if pads else []
        if side is not None:
            specs[side] = pl.BlockSpec(memory_space=pltpu.HBM if pin else pl.ANY)
            ins = [far(v) if pin and i == side else v for i, v in enumerate(ins)]
            scratch.append(pltpu.VMEM((27, ch, ch), BF16))
            if pads == 3:
                scratch.append(pltpu.VMEM((3, (depth + 2) * row, ch), BF16))
            scratch.append(pltpu.SemaphoreType.DMA((3,)))
        many = isinstance(outs, list)
        return pl.pallas_call(
            lambda *refs: kernel(*refs[:count], *refs[kept:]),
            out_shape=[jax.ShapeDtypeStruct((n, cells, ch), t) for n, t in outs] if many else outs,
            in_specs=specs,
            out_specs=[vmem] * len(outs) if many else vmem,
            scratch_shapes=scratch,
            compiler_params=pltpu.CompilerParams(vmem_limit_bytes=16 * 2**20),
        )(*ins, *map(far, deps))

    def forward(count, k, slices, base, first=(), deps=()):
        return call(
            functools.partial(forward_kernel, count, k, row),
            [info, *slices, weight_act, base, *first],
            [(count, BF16), (count + 1, BF16)] + [(5, BF16) for _ in first],
            3 * count,
            deps=deps,
        )

    def wide_back(k, cots, facs, *more, deps=()):
        last = {chips - 1: [(8, BF16)], 0: [(6, BF16), (2, BF16)]}.get(k, [])
        return call(
            functools.partial(wide_back_kernel, k, chips, row),
            [info, *cots, weight_act, *facs, *more],
            [(3, BF16), (5, BF16), *last],
            9,
            deps=deps,
        )

    def narrow_back(k, got, keep, *more, deps=()):
        return call(
            functools.partial(narrow_back_kernel, k, row),
            [info, got, keep, weight_act, *more],
            [(1, F32 if k == 0 else BF16), (3, BF16)],
            3,
            6 if k == 0 else None,
            deps,
        )

    def side_part(first, last, *sides):
        def run(weight, bias, *sides):
            return call(
                functools.partial(side_kernel, row, len(sides) == 5),
                [info, *sides, weight, bias],
                [(3, F32)],
                9,
                1 + len(sides),
            )[0]

        def skip(weight, bias, *sides):
            return jnp.zeros((3, cells, ch), F32)

        return lax.cond((section >= first) & (section <= last), run, skip, weight, bias, *sides)

    def side_back(first, last, odd, even):
        def run(weight, odd, even):
            return call(
                functools.partial(side_back_kernel, row), [info, odd, even, weight], [(3, BF16)], 9, 3
            )[0]

        def skip(weight, odd, even):
            return jnp.zeros((3, cells, ch), BF16)

        return lax.cond((section >= first) & (section <= last), run, skip, weight, odd, even)

    def sibling(block):
        return lax.ppermute(block, "section", [(s, s ^ 1) for s in range(sections)])

    def across(block, d, *pairs):
        route = [
            (s * spaces + i, t * spaces + (i + d) % spaces) for s, t in pairs for i in range(spaces)
        ]
        return lax.ppermute(block, BOTH, route)

    def hop(block, chip):
        pairs = [[(1, 2), (6, 5)], [(3, 4), (2, 1)], [(5, 6), (4, 3)]][chip]
        moved = {d: across(block, d, *pairs) for d in (2, -2, 1, -1, 0)}
        return [moved[d] for d in (2, 1, 0, -1, -2)]

    def halves(block):
        got = []
        for d in (2, 1):
            route = []
            for s in range(sections):
                move = d if s % 2 == 0 else -d
                route += [
                    (s * spaces + i, s * spaces + (i + move) % spaces) for i in range(spaces)
                ]
            got.append(lax.ppermute(block, BOTH, route))
        return got

    def along(block, *pairs):
        return lax.ppermute(block, "section", pairs)

    def after(value, *others):
        return lax.optimization_barrier((value, *others))[0]

    own = features.reshape(1, cells, ch)
    cot_own = cotangent.reshape(1, cells, ch)
    pair = call(pack_kernel, [own, cot_own], [(2, BF16)], 0)[0]
    got = halves(pair)
    other = [sibling(g) for g in got]
    act = [got[0], got[1], own, other[1], other[0]]
    cot = [other[0], other[1], cot_own, got[1], got[0]]

    base3 = side_part(1, half - 1, *act)
    deps = [base3]
    keeps3, keeps1 = [], []
    for k in range(chips):
        base = bias if k in (0, half // 2) else base3
        if k == 1:
            out3, keep3, act5 = forward(3, k, act, base, [first3])
        else:
            out3, keep3 = forward(3, k, act, base, deps=deps)
        in3 = sibling(out3)
        keeps3.append(keep3)
        deps = []
        if k == chips - 1:
            keep3 = sum(keeps3[1:], keeps3[0])
            fac_even = sibling(keep3)
        out1, keep1 = forward(1, k, [in3], base3, deps=deps)
        keeps1.append(keep1)
        if k == 0:
            first3 = out3
        if k + 1 < chips:
            act = hop(out1, k)
        if k == 1:
            moved3 = along(after(out3, keep1), (0, 7), (2, 5))
            moved5 = along(after(act5, keep1), (2, 6))
            base3 = side_part(half + 1, sections - 1, moved5, moved3)
        deps = [base3] if k == 1 else []
    keep1 = sum(keeps1[1:], keeps1[0])

    fac1 = keep1[:1]
    got = halves(jnp.where(core == 0, sibling(fac1), fac1))
    other = [sibling(g) for g in got]
    facs = [other[0], other[1], fac1, got[1], got[0], fac_even]
    act_own = jnp.where(core == 0, keep3[3:], keep1[1:])
    late = jnp.where(core == 0, moved5[2:3], moved3[1:2])
    side_own = jnp.where(section < half, own, jnp.where(section == half, act_own, late))
    joined = jnp.concatenate([act_own[0], side_own[0]], 1)
    blocks = jnp.transpose(joined.reshape(cells, spaces, -1), (1, 0, 2))
    blocks = lax.all_to_all(blocks, "space", 0, 0, tiled=True).reshape(spaces, cells, -1)
    fac_even, blocks = lax.optimization_barrier((fac_even, blocks))
    facs[5] = fac_even
    slopes5, slopes3, deps = [], [], []
    for k in reversed(range(chips)):
        more = []
        if k == 0:
            more = [moved_7_6, even3, sum(slopes5[1:], slopes5[0])]
        send, slope5, *extra = wide_back(k, cot, facs if k == chips - 1 else [facs], *more, deps=deps)
        if k == chips - 1:
            facs = extra[0]
        got = sibling(send)
        if k == 0:
            down = [(q, q - 1) for q in range(1, sections, 2)]
            evens = {d: across(extra[0], d, *down) for d in (3, -3, 6, -6)}
            opposite = across(extra[1], 8, *down)
            back = side_back(2, 3, after(old5, slope5), old3)
            from_next = across(back[1] + sibling(back[1]), 0, (3, 4), (2, 1))
            deps = [*evens.values(), opposite, back]
            sent, slope3 = narrow_back(k, got, keep3, old3, slope5, weight, deps=deps)
            continue
        more, deps = [], []
        if k == 1:
            more = [skip_narrow, moved_7_6]
        if k == 2:
            back = side_back(half + 1, sections - 1, slopes5[0] + slope5, slopes3[0])
            moved_7_6 = along(back, (7, 1), (6, 2))
            skip_narrow = along(back, (5, 2))
            deps = [back]
        sent, slope3 = narrow_back(k, got, keep3, *more, deps=deps)
        deps = []
        slopes5.append(slope5)
        slopes3.append(slope3)
        cot = hop(sent, {3: 0, 2: 2, 1: 1}[k])
        if k == 1:
            old5 = sum(slopes5[1:], slopes5[0])
            old3 = sum(slopes3[1:], slopes3[0])
            even3 = sibling(old3)
            zero = jnp.zeros_like(blocks[:1])
            lower = jnp.concatenate([zero, blocks[:-1]], 0)
            upper = jnp.concatenate([blocks[1:], zero], 0)
            shifted = jnp.stack([lower, blocks, upper])
            start = (place - 1) % spaces
            shifted = lax.dynamic_slice_in_dim(
                jnp.concatenate([shifted, shifted], 1), start, spaces, axis=1
            )
            shifted = jnp.transpose(shifted.reshape(3, spaces * cells, -1), (0, 2, 1))
            window = call(
                functools.partial(lambda r, i, *refs: window_kernel(r, *refs), row),
                [info, shifted],
                jax.ShapeDtypeStruct((27, shifted.shape[1], spaces * cells), BF16),
                0,
            )
            deps = [window]

    odds = {d: sibling(evens[d]) for d in evens}
    back_opposite = sibling(opposite)

    term = (sent[0] + jnp.where(section == 1, from_next, 0).astype(F32)).astype(BF16)
    width = ch // chips
    pieces = [term[:, j * width : (j + 1) * width] for j in range(chips)]
    piece = pieces[0]
    for j in (2, 1, 3):
        moved = along(pieces[j], (0, 2 * j), (1, 2 * j + 1))
        piece = jnp.where(chip == j, moved, piece)
    lower, upper = piece[:, : width // 2], piece[:, width // 2 :]
    moved = sibling(jnp.where(core == 0, upper, lower))
    grad_features = jnp.where(core == 0, lower, upper).astype(F32) + moved.astype(F32)

    even_pieces = [slope3, evens[-3], evens[-6], opposite, evens[6], evens[3]]
    odd_pieces = [slope5, odds[-3], odds[-6], back_opposite, odds[6], odds[3]]
    pieces = [*even_pieces, *odd_pieces]
    anywhere = pl.BlockSpec(memory_space=pltpu.HBM)
    grad_weight = pl.pallas_call(
        functools.partial(weight_grad_kernel, [len(even_pieces), len(odd_pieces)]),
        out_shape=jax.ShapeDtypeStruct((27, window.shape[1], ch), F32),
        in_specs=[smem] + [anywhere] * (1 + len(pieces)),
        out_specs=vmem,
        scratch_shapes=[
            pltpu.VMEM(window.shape, BF16),
            pltpu.VMEM((spaces, cells, ch), BF16),
            pltpu.SemaphoreType.DMA((3 + len(even_pieces),)),
        ],
        compiler_params=pltpu.CompilerParams(vmem_limit_bytes=24 * 2**20),
    )(info, far(window), *map(far, pieces))
    return (
        grad_features.reshape(1, depth, row, -1),
        jnp.transpose(grad_weight, (1, 0, 2))[None],
    )


def solution(mesh):
    return jax.shard_map(
        shards,
        mesh=mesh,
        in_specs=(
            P("space", None, None, None),
            P("section", None, None, None),
            P("section", None),
            P("space", None, None, None),
        ),
        out_specs=(P("space", None, None, "section"), P("section", "space", None, None)),
        check_vma=False,
    )
```

```python
import functools

import jax
import jax.numpy as jnp
from jax import lax
from jax.experimental import pallas as pl
from jax.experimental.pallas import tpu as pltpu
from jax.sharding import PartitionSpec as P

BF16 = jnp.bfloat16
F32 = jnp.float32
TAPS = [(a, b) for a in range(3) for b in range(3)]
BOTH = ("section", "space")
CORE, SECTION, LOW, HIGH = 0, 1, 2, 5


def fill(pad, info, slices, count, row):
    zero = jnp.zeros((pad.shape[0], row, pad.shape[2]), BF16)
    pad[:, :row, :] = zero
    pad[:, pad.shape[1] - row :, :] = zero
    first = 1 if count == 1 else 0
    for j in range(count):
        low = info[LOW + first + j] > 0
        high = info[HIGH + first + j] > 0
        values = [
            jnp.where(low, slices[j], jnp.zeros_like(slices[j])),
            slices[j + 1],
            jnp.where(high, slices[j + 2], jnp.zeros_like(slices[j])),
        ]
        for a in range(3):
            pad[a * count + j, row : pad.shape[1] - row, :] = values[a]


def shift_sum(low, mid, high, row):
    rows = mid.shape[0]
    y = lax.broadcasted_iota(jnp.int32, mid.shape, 0) % row
    low = jnp.where(y == 0, 0.0, pltpu.roll(low, 1, 0))
    high = jnp.where(y == row - 1, 0.0, pltpu.roll(high, rows - 1, 0))
    return mid + low + high


def taps_of(pad, first, w_ref, c, taps, count, row, flip):
    ch = pad.shape[2]
    cells = pad.shape[1] - 2 * row
    total = None
    for a, b in taps:
        lhs = pad[pl.ds(first + a * count, count), b * row : b * row + cells, :]
        tap = 9 * a + 3 * b + c
        if flip:
            tap = w_ref.shape[0] - 1 - tap
        part = lax.dot_general(
            lhs.reshape(count * cells, ch),
            w_ref[tap],
            (((1,), (1 if flip else 0,)), ((), ())),
            preferred_element_type=F32,
        )
        total = part if total is None else total + part
    return total


def conv(pad, w_ref, count, row, flip):
    parts = [taps_of(pad, 0, w_ref, c, TAPS, count, row, flip) for c in range(3)]
    return shift_sum(*parts, row).reshape(count, -1, pad.shape[2])


def conv_loop(pad, w_ref, count, row, flip):
    ch = pad.shape[2]
    cells = pad.shape[1] - 2 * row

    def step(a, parts):
        new = list(parts)
        for b in range(3):
            lhs = pad[pl.ds(a * count, count), b * row : b * row + cells, :]
            lhs = lhs.reshape(count * cells, ch)
            for c in range(3):
                tap = 9 * a + 3 * b + c
                if flip:
                    tap = 26 - tap
                new[c] = new[c] + lax.dot_general(
                    lhs,
                    w_ref[tap],
                    (((1,), (1 if flip else 0,)), ((), ())),
                    preferred_element_type=F32,
                )
        return tuple(new)

    zero = jnp.zeros((count * cells, ch), F32)
    parts = lax.fori_loop(0, 3, step, (zero, zero, zero))
    return shift_sum(*parts, row).reshape(count, cells, ch)


def pack_kernel(*refs):
    for i, ref in enumerate(refs[:-1]):
        refs[-1][i : i + 1] = ref[...]


def forward_kernel(count, k, row, info, *refs):
    cut = 5 if count == 3 else 1
    slices, refs = refs[:cut], refs[cut:]
    w_ref, base_ref, refs = refs[0], refs[1], refs[2:]
    wide = count == 3 and k == 1
    if wide:
        first_ref, refs = refs[0], refs[1:]
    out_ref, keep_ref, refs = refs[0], refs[1], refs[2:]
    if wide:
        all_ref, refs = refs[0], refs[1:]
    pad = refs[0]
    own = info[SECTION] == 2 * k + (0 if count == 3 else 1)

    @pl.when(own)
    def _():
        values = [s[0] for s in slices] if count == 3 else [slices[0][i] for i in range(3)]
        fill(pad, info, values, count, row)
        base = base_ref[...]
        if count == 1 and base.shape[0] == 3:
            base = base[1:2]
        preact = conv(pad, w_ref, count, row, False) + base
        logistic = jax.nn.sigmoid(preact)
        act = jnp.stack(values[1 : 1 + count]).astype(F32)
        out_ref[...] = (act + preact * logistic).astype(BF16)
        keep_ref[:count] = (logistic * (1.0 + preact * (1.0 - logistic))).astype(BF16)
        keep_ref[count] = values[2] if count == 3 else values[1]

    @pl.when(jnp.logical_not(own))
    def _():
        keep_ref[...] = jnp.zeros_like(keep_ref)
        out_ref[...] = first_ref[...] if wide else jnp.zeros_like(out_ref)

    if wide:
        for i in range(5):
            all_ref[i] = slices[i][0]


def wide_back_kernel(k, chips, row, info, *refs):
    cots, refs = refs[:5], refs[5:]
    w_ref, refs = refs[0], refs[1:]
    if k == chips - 1:
        facs, refs = refs[:6], refs[6:]
    else:
        facs_ref, refs = refs[0], refs[1:]
    if k == 0:
        skip_ref, even_old, slope_old, refs = refs[0], refs[1], refs[2], refs[3:]
    send_ref, slope_ref, refs = refs[0], refs[1], refs[2:]
    if k == chips - 1:
        extra_ref, refs = refs[0], refs[1:]
    if k == 0:
        even_ref, pair_ref, refs = refs[0], refs[1], refs[2:]
    pad = refs[0]
    own = info[SECTION] == 2 * k + 1
    if k == chips - 1:
        for i in range(5):
            extra_ref[i] = facs[i][0]
        extra_ref[5:] = facs[5][:3]

    @pl.when(own)
    def _():
        cot = [c[c.shape[0] - 1].astype(F32) for c in cots]
        fac = [f[0] for f in facs[:5]] if k == chips - 1 else [facs_ref[i] for i in range(5)]
        slope = [(c * f.astype(F32)).astype(BF16) for c, f in zip(cot, fac)]
        for i in range(5):
            slope_ref[i] = slope[i]
        fill(pad, info, slope, 3, row)
        sent = (jnp.stack(cot[1:4]) + conv(pad, w_ref, 3, row, True)).astype(BF16)
        if k == 0:
            sent = (sent.astype(F32) + skip_ref[...].astype(F32)).astype(BF16)
            even = (sent.astype(F32) * facs_ref[5:].astype(F32)).astype(BF16)
            even_ref[:3] = even
            for i in range(3):
                even_ref[3 + i] = slope[1 + i]
            pair_ref[0] = even[1]
            pair_ref[1] = slope[2]
        send_ref[...] = sent

    @pl.when(jnp.logical_not(own))
    def _():
        send_ref[...] = jnp.zeros_like(send_ref)
        if k == 0:
            slope_ref[...] = slope_old[...]
            even_ref[:3] = even_old[...]
            even_ref[3:] = slope_old[1:4]
            pair_ref[0] = even_old[1]
            pair_ref[1] = slope_old[2]
        else:
            slope_ref[...] = jnp.zeros_like(slope_ref)


def narrow_back_kernel(k, row, info, *refs):
    got_ref, keep_ref, w_ref, refs = refs[0], refs[1], refs[2], refs[3:]
    if k == 1:
        skip_ref, next_ref, refs = refs[0], refs[1], refs[2:]
    if k == 0:
        (slope_old, odd_ref, w_hbm), refs = refs[:3], refs[3:]
    sent_ref, slope_ref, refs = refs[0], refs[1], refs[2:]
    if k == 0:
        pad, w_side, pad_side, sems = refs
    else:
        pad = refs[0]

    @pl.when(info[SECTION] == 2 * k)
    def _():
        cot = got_ref[...]
        if k == 1:
            cot = (cot.astype(F32) + skip_ref[...].astype(F32)).astype(BF16)
        slope = (cot.astype(F32) * keep_ref[:3].astype(F32)).astype(BF16)
        slope_ref[...] = slope
        fill(pad, info, [slope[i] for i in range(3)], 1, row)
        total = cot[1:2].astype(F32) + conv(pad, w_ref, 1, row, True)
        if k == 1:
            total = total + next_ref[1:2].astype(F32)
        sent_ref[...] = total.astype(sent_ref.dtype)

    @pl.when(info[SECTION] != 2 * k)
    def _():
        slope_ref[...] = slope_old[...] if k == 0 else jnp.zeros_like(slope_ref)
        if k == 0:

            @pl.when(info[SECTION] == 1)
            def _():
                values = [odd_ref[i] for i in range(1, 4)]
                sent_ref[...] = side_conv(values, True, row, info, w_hbm, pad_side, w_side, sems, 1)

            @pl.when(info[SECTION] > 1)
            def _():
                sent_ref[...] = jnp.zeros_like(sent_ref)

        else:
            sent_ref[...] = jnp.zeros_like(sent_ref)


def side_conv(values, flip, row, info, w_hbm, pad, w_ref, sems, count=3):
    ch = pad.shape[2]
    copies = []
    for i in range(3):
        taps = pl.ds(9 * i, 9)
        copy = pltpu.make_async_copy(w_hbm.at[taps, pl.ds(ch, ch)], w_ref.at[taps], sems.at[i])
        copies.append(copy)
    for copy in copies:
        copy.start()
    fill(pad, info, values, count, row)
    for copy in copies:
        copy.wait()
    if flip:
        return conv(pad, w_ref, count, row, flip)
    return conv_loop(pad, w_ref, count, row, flip)


def side_kernel(row, early, info, *refs):
    count = 5 if early else 2
    sides, (w_hbm, bias_ref, out_ref, pad, w_ref, sems) = refs[:count], refs[count:]
    if early:
        got = [s[0] for s in sides]
        values = [jnp.where(info[CORE] == 0, got[i], got[4 - i]) for i in range(5)]
    else:
        five, three = sides
        zero = jnp.zeros_like(five[0])
        rest = [zero, three[0], three[1], three[2], zero]
        values = [jnp.where(info[CORE] == 0, five[i], rest[i]) for i in range(5)]
    out_ref[...] = side_conv(values, False, row, info, w_hbm, pad, w_ref, sems) + bias_ref[...]


def side_back_kernel(row, info, odd_ref, even_ref, w_hbm, out_ref, pad, w_ref, sems):
    zero = jnp.zeros_like(even_ref[0])
    even = [zero, even_ref[0], even_ref[1], even_ref[2], zero]
    values = [jnp.where(info[CORE] == 1, odd_ref[i], even[i]) for i in range(5)]
    out_ref[...] = side_conv(values, True, row, info, w_hbm, pad, w_ref, sems).astype(BF16)


def window_kernel(row, joined_ref, out_ref):
    cells = joined_ref.shape[2]
    cell = lax.broadcasted_iota(jnp.int32, joined_ref.shape[1:], 1)
    z = cell // row % 4
    y = cell % row
    for a in range(3):
        value = joined_ref[a].astype(F32)
        for b, c in TAPS:
            move = (b - 1) * row + (c - 1)
            part = value if move == 0 else pltpu.roll(value, (-move) % cells, 1)
            valid = (z + b - 1 >= 0) & (z + b - 1 < 4) & (y + c - 1 >= 0) & (y + c - 1 < row)
            out_ref[9 * a + 3 * b + c] = jnp.where(valid, part, 0.0).astype(BF16)


def weight_grad_kernel(counts, info, window_hbm, *refs):
    out_ref, window_ref, slopes_ref, sems = refs[-4:]
    taps, rows, cells = window_ref.shape
    ch = slopes_ref.shape[2]
    lanes = [
        pltpu.make_async_copy(window_hbm.at[pl.ds(9 * a, 9)], window_ref.at[pl.ds(9 * a, 9)], sems.at[a])
        for a in range(3)
    ]
    for copy in lanes:
        copy.start()
    start = 0
    for kind, count in enumerate(counts):
        pieces = refs[start : start + count]
        start += count

        @pl.when(info[CORE] == kind)
        def _():
            copies, place = [], 0
            for i, piece in enumerate(pieces):
                size = 1 if piece.shape[0] == 2 else 3
                first = {2: kind, 3: 0, 5: 1, 6: 3 * kind}[piece.shape[0]]
                source = piece.at[pl.ds(first, size)]
                target = slopes_ref.at[pl.ds(place, size)]
                copies.append(pltpu.make_async_copy(source, target, sems.at[3 + i]))
                place += size
            for copy in copies:
                copy.start()
            for copy in copies:
                copy.wait()

    slopes = slopes_ref[...].reshape(cells, ch)
    for a in range(3):
        lanes[a].wait()
        lhs = window_ref[9 * a : 9 * a + 9].reshape(9 * rows, cells)
        grad = jnp.dot(lhs, slopes, preferred_element_type=F32)
        out_ref[9 * a : 9 * a + 9] = grad.reshape(9, rows, -1)


def shards(features, section_weight, section_bias, cotangent):
    sections = lax.axis_size("section")
    spaces = lax.axis_size("space")
    half = sections // 2
    chips = sections // 2
    section = lax.axis_index("section")
    place = lax.axis_index("space")
    chip, core = section // 2, section % 2
    _, depth, row, ch = features.shape
    cells = depth * row

    weight = jnp.transpose(section_weight[0], (1, 0, 2))
    doubled = (section == 0) | (section == half)
    weight_act = weight[:, :ch]
    weight_act = jnp.where(
        doubled, (weight_act.astype(F32) + weight[:, ch:].astype(F32)).astype(BF16), weight_act
    )
    bias = section_bias.reshape(1, 1, ch)
    at = (place + jnp.arange(-1, 2)) % spaces
    info = jnp.concatenate(
        [jnp.stack([core, section]), (at > 0), (at < spaces - 1)]
    ).astype(jnp.int32)
    vmem = pl.BlockSpec(memory_space=pltpu.VMEM)
    smem = pl.BlockSpec(memory_space=pltpu.SMEM)

    def far(value):
        return pltpu.with_memory_space_constraint(value, pltpu.HBM)

    def call(kernel, ins, outs, pads, side=None, deps=(), pin=False):
        count, kept = len(ins), len(ins) + len(deps)
        specs = [vmem if i or kernel is pack_kernel else smem for i in range(count)]
        specs += [pl.BlockSpec(memory_space=pltpu.HBM)] * len(deps)
        scratch = [pltpu.VMEM((pads, (depth + 2) * row, ch), BF16)] if pads else []
        if side is not None:
            specs[side] = pl.BlockSpec(memory_space=pltpu.HBM if pin else pl.ANY)
            ins = [far(v) if pin and i == side else v for i, v in enumerate(ins)]
            scratch.append(pltpu.VMEM((27, ch, ch), BF16))
            if pads == 3:
                scratch.append(pltpu.VMEM((3, (depth + 2) * row, ch), BF16))
            scratch.append(pltpu.SemaphoreType.DMA((3,)))
        many = isinstance(outs, list)
        return pl.pallas_call(
            lambda *refs: kernel(*refs[:count], *refs[kept:]),
            out_shape=[jax.ShapeDtypeStruct((n, cells, ch), t) for n, t in outs] if many else outs,
            in_specs=specs,
            out_specs=[vmem] * len(outs) if many else vmem,
            scratch_shapes=scratch,
            compiler_params=pltpu.CompilerParams(vmem_limit_bytes=16 * 2**20),
        )(*ins, *map(far, deps))

    def forward(count, k, slices, base, first=(), deps=()):
        return call(
            functools.partial(forward_kernel, count, k, row),
            [info, *slices, weight_act, base, *first],
            [(count, BF16), (count + 1, BF16)] + [(5, BF16) for _ in first],
            3 * count,
            deps=deps,
        )

    def wide_back(k, cots, facs, *more, deps=()):
        last = {chips - 1: [(8, BF16)], 0: [(6, BF16), (2, BF16)]}.get(k, [])
        return call(
            functools.partial(wide_back_kernel, k, chips, row),
            [info, *cots, weight_act, *facs, *more],
            [(3, BF16), (5, BF16), *last],
            9,
            deps=deps,
        )

    def narrow_back(k, got, keep, *more, deps=()):
        return call(
            functools.partial(narrow_back_kernel, k, row),
            [info, got, keep, weight_act, *more],
            [(1, F32 if k == 0 else BF16), (3, BF16)],
            3,
            6 if k == 0 else None,
            deps,
        )

    def side_part(first, last, *sides):
        def run(weight, bias, *sides):
            return call(
                functools.partial(side_kernel, row, len(sides) == 5),
                [info, *sides, weight, bias],
                [(3, F32)],
                9,
                1 + len(sides),
            )[0]

        def skip(weight, bias, *sides):
            return jnp.zeros((3, cells, ch), F32)

        return lax.cond((section >= first) & (section <= last), run, skip, weight, bias, *sides)

    def side_back(first, last, odd, even):
        def run(weight, odd, even):
            return call(
                functools.partial(side_back_kernel, row), [info, odd, even, weight], [(3, BF16)], 9, 3
            )[0]

        def skip(weight, odd, even):
            return jnp.zeros((3, cells, ch), BF16)

        return lax.cond((section >= first) & (section <= last), run, skip, weight, odd, even)

    def sibling(block):
        return lax.ppermute(block, "section", [(s, s ^ 1) for s in range(sections)])

    def across(block, d, *pairs):
        route = [
            (s * spaces + i, t * spaces + (i + d) % spaces) for s, t in pairs for i in range(spaces)
        ]
        return lax.ppermute(block, BOTH, route)

    def hop(block, chip):
        pairs = [[(1, 2), (6, 5)], [(3, 4), (2, 1)], [(5, 6), (4, 3)]][chip]
        moved = {d: across(block, d, *pairs) for d in (2, -2, 1, -1, 0)}
        return [moved[d] for d in (2, 1, 0, -1, -2)]

    def halves(block):
        got = []
        for d in (2, 1):
            route = []
            for s in range(sections):
                move = d if s % 2 == 0 else -d
                route += [
                    (s * spaces + i, s * spaces + (i + move) % spaces) for i in range(spaces)
                ]
            got.append(lax.ppermute(block, BOTH, route))
        return got

    def along(block, *pairs):
        return lax.ppermute(block, "section", pairs)

    def after(value, *others):
        return lax.optimization_barrier((value, *others))[0]

    own = features.reshape(1, cells, ch)
    cot_own = cotangent.reshape(1, cells, ch)
    pair = call(pack_kernel, [own, cot_own], [(2, BF16)], 0)[0]
    got = halves(pair)
    other = [sibling(g) for g in got]
    act = [got[0], got[1], own, other[1], other[0]]
    cot = [other[0], other[1], cot_own, got[1], got[0]]

    base3 = side_part(1, half - 1, *act)
    deps = [base3]
    keeps3, keeps1 = [], []
    for k in range(chips):
        base = bias if k in (0, half // 2) else base3
        if k == 1:
            out3, keep3, act5 = forward(3, k, act, base, [first3])
        else:
            out3, keep3 = forward(3, k, act, base, deps=deps)
        in3 = sibling(out3)
        keeps3.append(keep3)
        deps = []
        if k == chips - 1:
            keep3 = sum(keeps3[1:], keeps3[0])
            fac_even = sibling(keep3)
        out1, keep1 = forward(1, k, [in3], base3, deps=deps)
        keeps1.append(keep1)
        if k == 0:
            first3 = out3
        if k + 1 < chips:
            act = hop(out1, k)
        if k == 1:
            moved3 = along(after(out3, keep1), (0, 7), (2, 5))
            moved5 = along(after(act5, keep1), (2, 6))
            base3 = side_part(half + 1, sections - 1, moved5, moved3)
        deps = [base3] if k == 1 else []
    keep1 = sum(keeps1[1:], keeps1[0])

    fac1 = keep1[:1]
    got = halves(jnp.where(core == 0, sibling(fac1), fac1))
    other = [sibling(g) for g in got]
    facs = [other[0], other[1], fac1, got[1], got[0], fac_even]
    act_own = jnp.where(core == 0, keep3[3:], keep1[1:])
    late = jnp.where(core == 0, moved5[2:3], moved3[1:2])
    side_own = jnp.where(section < half, own, jnp.where(section == half, act_own, late))
    joined = jnp.concatenate([act_own[0], side_own[0]], 1)
    blocks = jnp.transpose(joined.reshape(cells, spaces, -1), (1, 0, 2))
    blocks = lax.all_to_all(blocks, "space", 0, 0, tiled=True).reshape(spaces, cells, -1)
    fac_even, blocks = lax.optimization_barrier((fac_even, blocks))
    facs[5] = fac_even
    slopes5, slopes3, deps = [], [], []
    for k in reversed(range(chips)):
        more = []
        if k == 0:
            more = [moved_7_6, even3, sum(slopes5[1:], slopes5[0])]
        send, slope5, *extra = wide_back(k, cot, facs if k == chips - 1 else [facs], *more, deps=deps)
        if k == chips - 1:
            facs = extra[0]
        got = sibling(send)
        if k == 0:
            down = [(q, q - 1) for q in range(1, sections, 2)]
            evens = {d: across(extra[0], d, *down) for d in (3, -3, 6, -6)}
            opposite = across(extra[1], 8, *down)
            back = side_back(2, 3, after(old5, slope5), old3)
            from_next = across(back[1] + sibling(back[1]), 0, (3, 4), (2, 1))
            deps = [*evens.values(), opposite, back]
            sent, slope3 = narrow_back(k, got, keep3, old3, slope5, weight, deps=deps)
            continue
        more, deps = [], []
        if k == 1:
            more = [skip_narrow, moved_7_6]
        if k == 2:
            back = side_back(half + 1, sections - 1, slopes5[0] + slope5, slopes3[0])
            moved_7_6 = along(back, (7, 1), (6, 2))
            skip_narrow = along(back, (5, 2))
            deps = [back]
        sent, slope3 = narrow_back(k, got, keep3, *more, deps=deps)
        deps = []
        slopes5.append(slope5)
        slopes3.append(slope3)
        cot = hop(sent, {3: 0, 2: 2, 1: 1}[k])
        if k == 1:
            old5 = sum(slopes5[1:], slopes5[0])
            old3 = sum(slopes3[1:], slopes3[0])
            even3 = sibling(old3)
            zero = jnp.zeros_like(blocks[:1])
            lower = jnp.concatenate([zero, blocks[:-1]], 0)
            upper = jnp.concatenate([blocks[1:], zero], 0)
            shifted = jnp.stack([lower, blocks, upper])
            start = (place - 1) % spaces
            shifted = lax.dynamic_slice_in_dim(
                jnp.concatenate([shifted, shifted], 1), start, spaces, axis=1
            )
            shifted = jnp.transpose(shifted.reshape(3, spaces * cells, -1), (0, 2, 1))
            window = call(
                functools.partial(lambda r, i, *refs: window_kernel(r, *refs), row),
                [info, shifted],
                jax.ShapeDtypeStruct((27, shifted.shape[1], spaces * cells), BF16),
                0,
            )
            deps = [window]

    odds = {d: sibling(evens[d]) for d in evens}
    back_opposite = sibling(opposite)

    term = (sent[0] + jnp.where(section == 1, from_next, 0).astype(F32)).astype(BF16)
    width = ch // chips
    pieces = [term[:, j * width : (j + 1) * width] for j in range(chips)]
    piece = pieces[0]
    for j in (2, 1, 3):
        moved = along(pieces[j], (0, 2 * j), (1, 2 * j + 1))
        piece = jnp.where(chip == j, moved, piece)
    lower, upper = piece[:, : width // 2], piece[:, width // 2 :]
    moved = sibling(jnp.where(core == 0, upper, lower))
    grad_features = jnp.where(core == 0, lower, upper).astype(F32) + moved.astype(F32)

    even_pieces = [slope3, evens[-3], evens[-6], opposite, evens[6], evens[3]]
    odd_pieces = [slope5, odds[-3], odds[-6], back_opposite, odds[6], odds[3]]
    pieces = [*even_pieces, *odd_pieces]
    anywhere = pl.BlockSpec(memory_space=pltpu.HBM)
    grad_weight = pl.pallas_call(
        functools.partial(weight_grad_kernel, [len(even_pieces), len(odd_pieces)]),
        out_shape=jax.ShapeDtypeStruct((27, window.shape[1], ch), F32),
        in_specs=[smem] + [anywhere] * (1 + len(pieces)),
        out_specs=vmem,
        scratch_shapes=[
            pltpu.VMEM(window.shape, BF16),
            pltpu.VMEM((spaces, cells, ch), BF16),
            pltpu.SemaphoreType.DMA((3 + len(even_pieces),)),
        ],
        compiler_params=pltpu.CompilerParams(vmem_limit_bytes=24 * 2**20),
    )(info, far(window), *map(far, pieces))
    return (
        grad_features.reshape(1, depth, row, -1),
        jnp.transpose(grad_weight, (1, 0, 2))[None],
    )


def solution(mesh):
    return jax.shard_map(
        shards,
        mesh=mesh,
        in_specs=(
            P("space", None, None, None),
            P("section", None, None, None),
            P("section", None),
            P("space", None, None, None),
        ),
        out_specs=(P("space", None, None, "section"), P("section", "space", None, None)),
        check_vma=False,
    )
```

```python
import functools

import jax
import jax.numpy as jnp
from jax import lax
from jax.experimental import pallas as pl
from jax.experimental.pallas import tpu as pltpu
from jax.sharding import PartitionSpec as P

BF16 = jnp.bfloat16
F32 = jnp.float32
TAPS = [(a, b) for a in range(3) for b in range(3)]
BOTH = ("section", "space")
CORE, SECTION, LOW, HIGH = 0, 1, 2, 5


def fill(pad, info, slices, count, row):
    zero = jnp.zeros((pad.shape[0], row, pad.shape[2]), BF16)
    pad[:, :row, :] = zero
    pad[:, pad.shape[1] - row :, :] = zero
    first = 1 if count == 1 else 0
    for j in range(count):
        low = info[LOW + first + j] > 0
        high = info[HIGH + first + j] > 0
        values = [
            jnp.where(low, slices[j], jnp.zeros_like(slices[j])),
            slices[j + 1],
            jnp.where(high, slices[j + 2], jnp.zeros_like(slices[j])),
        ]
        for a in range(3):
            pad[a * count + j, row : pad.shape[1] - row, :] = values[a]


def shift_sum(low, mid, high, row):
    rows = mid.shape[0]
    y = lax.broadcasted_iota(jnp.int32, mid.shape, 0) % row
    low = jnp.where(y == 0, 0.0, pltpu.roll(low, 1, 0))
    high = jnp.where(y == row - 1, 0.0, pltpu.roll(high, rows - 1, 0))
    return mid + low + high


def taps_of(pad, first, w_ref, c, taps, count, row, flip):
    ch = pad.shape[2]
    cells = pad.shape[1] - 2 * row
    total = None
    for a, b in taps:
        lhs = pad[pl.ds(first + a * count, count), b * row : b * row + cells, :]
        tap = 9 * a + 3 * b + c
        if flip:
            tap = w_ref.shape[0] - 1 - tap
        part = lax.dot_general(
            lhs.reshape(count * cells, ch),
            w_ref[tap],
            (((1,), (1 if flip else 0,)), ((), ())),
            preferred_element_type=F32,
        )
        total = part if total is None else total + part
    return total


def conv(pad, w_ref, count, row, flip):
    parts = [taps_of(pad, 0, w_ref, c, TAPS, count, row, flip) for c in range(3)]
    return shift_sum(*parts, row).reshape(count, -1, pad.shape[2])


def conv_loop(pad, w_ref, count, row, flip):
    ch = pad.shape[2]
    cells = pad.shape[1] - 2 * row

    def step(a, parts):
        new = list(parts)
        for b in range(3):
            lhs = pad[pl.ds(a * count, count), b * row : b * row + cells, :]
            lhs = lhs.reshape(count * cells, ch)
            for c in range(3):
                tap = 9 * a + 3 * b + c
                if flip:
                    tap = 26 - tap
                new[c] = new[c] + lax.dot_general(
                    lhs,
                    w_ref[tap],
                    (((1,), (1 if flip else 0,)), ((), ())),
                    preferred_element_type=F32,
                )
        return tuple(new)

    zero = jnp.zeros((count * cells, ch), F32)
    parts = lax.fori_loop(0, 3, step, (zero, zero, zero))
    return shift_sum(*parts, row).reshape(count, cells, ch)


def pack_kernel(*refs):
    for i, ref in enumerate(refs[:-1]):
        refs[-1][i : i + 1] = ref[...]


def forward_kernel(count, k, row, info, *refs):
    cut = 5 if count == 3 else 1
    slices, refs = refs[:cut], refs[cut:]
    w_ref, base_ref, refs = refs[0], refs[1], refs[2:]
    wide = count == 3 and k == 1
    if wide:
        first_ref, refs = refs[0], refs[1:]
    out_ref, keep_ref, refs = refs[0], refs[1], refs[2:]
    if wide:
        all_ref, refs = refs[0], refs[1:]
    pad = refs[0]
    own = info[SECTION] == 2 * k + (0 if count == 3 else 1)

    @pl.when(own)
    def _():
        values = [s[0] for s in slices] if count == 3 else [slices[0][i] for i in range(3)]
        fill(pad, info, values, count, row)
        base = base_ref[...]
        if count == 1 and base.shape[0] == 3:
            base = base[1:2]
        preact = conv(pad, w_ref, count, row, False) + base
        logistic = jax.nn.sigmoid(preact)
        act = jnp.stack(values[1 : 1 + count]).astype(F32)
        out_ref[...] = (act + preact * logistic).astype(BF16)
        keep_ref[:count] = (logistic * (1.0 + preact * (1.0 - logistic))).astype(BF16)
        keep_ref[count] = values[2] if count == 3 else values[1]

    @pl.when(jnp.logical_not(own))
    def _():
        keep_ref[...] = jnp.zeros_like(keep_ref)
        out_ref[...] = first_ref[...] if wide else jnp.zeros_like(out_ref)

    if wide:
        for i in range(5):
            all_ref[i] = slices[i][0]


def wide_back_kernel(k, chips, row, info, *refs):
    cots, refs = refs[:5], refs[5:]
    w_ref, refs = refs[0], refs[1:]
    if k == chips - 1:
        facs, refs = refs[:6], refs[6:]
    else:
        facs_ref, refs = refs[0], refs[1:]
    if k == 0:
        skip_ref, even_old, slope_old, refs = refs[0], refs[1], refs[2], refs[3:]
    send_ref, slope_ref, refs = refs[0], refs[1], refs[2:]
    if k == chips - 1:
        extra_ref, refs = refs[0], refs[1:]
    if k == 0:
        even_ref, pair_ref, refs = refs[0], refs[1], refs[2:]
    pad = refs[0]
    own = info[SECTION] == 2 * k + 1
    if k == chips - 1:
        for i in range(5):
            extra_ref[i] = facs[i][0]
        extra_ref[5:] = facs[5][:3]

    @pl.when(own)
    def _():
        cot = [c[c.shape[0] - 1].astype(F32) for c in cots]
        fac = [f[0] for f in facs[:5]] if k == chips - 1 else [facs_ref[i] for i in range(5)]
        slope = [(c * f.astype(F32)).astype(BF16) for c, f in zip(cot, fac)]
        for i in range(5):
            slope_ref[i] = slope[i]
        fill(pad, info, slope, 3, row)
        sent = (jnp.stack(cot[1:4]) + conv(pad, w_ref, 3, row, True)).astype(BF16)
        if k == 0:
            sent = (sent.astype(F32) + skip_ref[...].astype(F32)).astype(BF16)
            even = (sent.astype(F32) * facs_ref[5:].astype(F32)).astype(BF16)
            even_ref[:3] = even
            for i in range(3):
                even_ref[3 + i] = slope[1 + i]
            pair_ref[0] = even[1]
            pair_ref[1] = slope[2]
        send_ref[...] = sent

    @pl.when(jnp.logical_not(own))
    def _():
        send_ref[...] = jnp.zeros_like(send_ref)
        if k == 0:
            slope_ref[...] = slope_old[...]
            even_ref[:3] = even_old[...]
            even_ref[3:] = slope_old[1:4]
            pair_ref[0] = even_old[1]
            pair_ref[1] = slope_old[2]
        else:
            slope_ref[...] = jnp.zeros_like(slope_ref)


def narrow_back_kernel(k, row, info, *refs):
    got_ref, keep_ref, w_ref, refs = refs[0], refs[1], refs[2], refs[3:]
    if k == 1:
        skip_ref, next_ref, refs = refs[0], refs[1], refs[2:]
    if k == 0:
        (slope_old, odd_ref, w_hbm), refs = refs[:3], refs[3:]
    sent_ref, slope_ref, refs = refs[0], refs[1], refs[2:]
    if k == 0:
        pad, w_side, pad_side, sems = refs
    else:
        pad = refs[0]

    @pl.when(info[SECTION] == 2 * k)
    def _():
        cot = got_ref[...]
        if k == 1:
            cot = (cot.astype(F32) + skip_ref[...].astype(F32)).astype(BF16)
        slope = (cot.astype(F32) * keep_ref[:3].astype(F32)).astype(BF16)
        slope_ref[...] = slope
        fill(pad, info, [slope[i] for i in range(3)], 1, row)
        total = cot[1:2].astype(F32) + conv(pad, w_ref, 1, row, True)
        if k == 1:
            total = total + next_ref[1:2].astype(F32)
        sent_ref[...] = total.astype(sent_ref.dtype)

    @pl.when(info[SECTION] != 2 * k)
    def _():
        slope_ref[...] = slope_old[...] if k == 0 else jnp.zeros_like(slope_ref)
        if k == 0:

            @pl.when(info[SECTION] == 1)
            def _():
                values = [odd_ref[i] for i in range(1, 4)]
                sent_ref[...] = side_conv(values, True, row, info, w_hbm, pad_side, w_side, sems, 1)

            @pl.when(info[SECTION] > 1)
            def _():
                sent_ref[...] = jnp.zeros_like(sent_ref)

        else:
            sent_ref[...] = jnp.zeros_like(sent_ref)


def side_conv(values, flip, row, info, w_hbm, pad, w_ref, sems, count=3):
    ch = pad.shape[2]
    copies = []
    for i in range(3):
        taps = pl.ds(9 * i, 9)
        copy = pltpu.make_async_copy(w_hbm.at[taps, pl.ds(ch, ch)], w_ref.at[taps], sems.at[i])
        copies.append(copy)
    for copy in copies:
        copy.start()
    fill(pad, info, values, count, row)
    for copy in copies:
        copy.wait()
    if count == 1:
        return conv(pad, w_ref, count, row, flip)
    return conv_loop(pad, w_ref, count, row, flip)


def side_kernel(row, early, info, *refs):
    count = 5 if early else 2
    sides, (w_hbm, bias_ref, out_ref, pad, w_ref, sems) = refs[:count], refs[count:]
    if early:
        got = [s[0] for s in sides]
        values = [jnp.where(info[CORE] == 0, got[i], got[4 - i]) for i in range(5)]
    else:
        five, three = sides
        zero = jnp.zeros_like(five[0])
        rest = [zero, three[0], three[1], three[2], zero]
        values = [jnp.where(info[CORE] == 0, five[i], rest[i]) for i in range(5)]
    out_ref[...] = side_conv(values, False, row, info, w_hbm, pad, w_ref, sems) + bias_ref[...]


def side_back_kernel(row, info, odd_ref, even_ref, w_hbm, out_ref, pad, w_ref, sems):
    zero = jnp.zeros_like(even_ref[0])
    even = [zero, even_ref[0], even_ref[1], even_ref[2], zero]
    values = [jnp.where(info[CORE] == 1, odd_ref[i], even[i]) for i in range(5)]
    out_ref[...] = side_conv(values, True, row, info, w_hbm, pad, w_ref, sems).astype(BF16)


def window_kernel(row, joined_ref, out_ref):
    cells = joined_ref.shape[2]
    cell = lax.broadcasted_iota(jnp.int32, joined_ref.shape[1:], 1)
    z = cell // row % 4
    y = cell % row
    for a in range(3):
        value = joined_ref[a].astype(F32)
        for b, c in TAPS:
            move = (b - 1) * row + (c - 1)
            part = value if move == 0 else pltpu.roll(value, (-move) % cells, 1)
            valid = (z + b - 1 >= 0) & (z + b - 1 < 4) & (y + c - 1 >= 0) & (y + c - 1 < row)
            out_ref[9 * a + 3 * b + c] = jnp.where(valid, part, 0.0).astype(BF16)


def weight_grad_kernel(counts, info, window_hbm, *refs):
    out_ref, window_ref, slopes_ref, sems = refs[-4:]
    taps, rows, cells = window_ref.shape
    ch = slopes_ref.shape[2]
    lanes = [
        pltpu.make_async_copy(window_hbm.at[pl.ds(9 * a, 9)], window_ref.at[pl.ds(9 * a, 9)], sems.at[a])
        for a in range(3)
    ]
    for copy in lanes:
        copy.start()
    start = 0
    for kind, count in enumerate(counts):
        pieces = refs[start : start + count]
        start += count

        @pl.when(info[CORE] == kind)
        def _():
            copies, place = [], 0
            for i, piece in enumerate(pieces):
                size = 1 if piece.shape[0] == 2 else 3
                first = {2: kind, 3: 0, 5: 1, 6: 3 * kind}[piece.shape[0]]
                source = piece.at[pl.ds(first, size)]
                target = slopes_ref.at[pl.ds(place, size)]
                copies.append(pltpu.make_async_copy(source, target, sems.at[3 + i]))
                place += size
            for copy in copies:
                copy.start()
            for copy in copies:
                copy.wait()

    slopes = slopes_ref[...].reshape(cells, ch)
    for a in range(3):
        lanes[a].wait()
        lhs = window_ref[9 * a : 9 * a + 9].reshape(9 * rows, cells)
        grad = jnp.dot(lhs, slopes, preferred_element_type=F32)
        out_ref[9 * a : 9 * a + 9] = grad.reshape(9, rows, -1)


def shards(features, section_weight, section_bias, cotangent):
    sections = lax.axis_size("section")
    spaces = lax.axis_size("space")
    half = sections // 2
    chips = sections // 2
    section = lax.axis_index("section")
    place = lax.axis_index("space")
    chip, core = section // 2, section % 2
    _, depth, row, ch = features.shape
    cells = depth * row

    weight = jnp.transpose(section_weight[0], (1, 0, 2))
    doubled = (section == 0) | (section == half)
    weight_act = weight[:, :ch]
    weight_act = jnp.where(
        doubled, (weight_act.astype(F32) + weight[:, ch:].astype(F32)).astype(BF16), weight_act
    )
    bias = section_bias.reshape(1, 1, ch)
    at = (place + jnp.arange(-1, 2)) % spaces
    info = jnp.concatenate(
        [jnp.stack([core, section]), (at > 0), (at < spaces - 1)]
    ).astype(jnp.int32)
    vmem = pl.BlockSpec(memory_space=pltpu.VMEM)
    smem = pl.BlockSpec(memory_space=pltpu.SMEM)

    def far(value):
        return pltpu.with_memory_space_constraint(value, pltpu.HBM)

    def call(kernel, ins, outs, pads, side=None, deps=(), pin=False):
        count, kept = len(ins), len(ins) + len(deps)
        specs = [vmem if i or kernel is pack_kernel else smem for i in range(count)]
        specs += [pl.BlockSpec(memory_space=pltpu.HBM)] * len(deps)
        scratch = [pltpu.VMEM((pads, (depth + 2) * row, ch), BF16)] if pads else []
        if side is not None:
            specs[side] = pl.BlockSpec(memory_space=pltpu.HBM if pin else pl.ANY)
            ins = [far(v) if pin and i == side else v for i, v in enumerate(ins)]
            scratch.append(pltpu.VMEM((27, ch, ch), BF16))
            if pads == 3:
                scratch.append(pltpu.VMEM((3, (depth + 2) * row, ch), BF16))
            scratch.append(pltpu.SemaphoreType.DMA((3,)))
        many = isinstance(outs, list)
        return pl.pallas_call(
            lambda *refs: kernel(*refs[:count], *refs[kept:]),
            out_shape=[jax.ShapeDtypeStruct((n, cells, ch), t) for n, t in outs] if many else outs,
            in_specs=specs,
            out_specs=[vmem] * len(outs) if many else vmem,
            scratch_shapes=scratch,
            compiler_params=pltpu.CompilerParams(vmem_limit_bytes=16 * 2**20),
        )(*ins, *map(far, deps))

    def forward(count, k, slices, base, first=(), deps=()):
        return call(
            functools.partial(forward_kernel, count, k, row),
            [info, *slices, weight_act, base, *first],
            [(count, BF16), (count + 1, BF16)] + [(5, BF16) for _ in first],
            3 * count,
            deps=deps,
        )

    def wide_back(k, cots, facs, *more, deps=()):
        last = {chips - 1: [(8, BF16)], 0: [(6, BF16), (2, BF16)]}.get(k, [])
        return call(
            functools.partial(wide_back_kernel, k, chips, row),
            [info, *cots, weight_act, *facs, *more],
            [(3, BF16), (5, BF16), *last],
            9,
            deps=deps,
        )

    def narrow_back(k, got, keep, *more, deps=()):
        return call(
            functools.partial(narrow_back_kernel, k, row),
            [info, got, keep, weight_act, *more],
            [(1, F32 if k == 0 else BF16), (3, BF16)],
            3,
            6 if k == 0 else None,
            deps,
        )

    def side_part(first, last, *sides):
        def run(weight, bias, *sides):
            return call(
                functools.partial(side_kernel, row, len(sides) == 5),
                [info, *sides, weight, bias],
                [(3, F32)],
                9,
                1 + len(sides),
            )[0]

        def skip(weight, bias, *sides):
            return jnp.zeros((3, cells, ch), F32)

        return lax.cond((section >= first) & (section <= last), run, skip, weight, bias, *sides)

    def side_back(first, last, odd, even):
        def run(weight, odd, even):
            return call(
                functools.partial(side_back_kernel, row), [info, odd, even, weight], [(3, BF16)], 9, 3
            )[0]

        def skip(weight, odd, even):
            return jnp.zeros((3, cells, ch), BF16)

        return lax.cond((section >= first) & (section <= last), run, skip, weight, odd, even)

    def sibling(block):
        return lax.ppermute(block, "section", [(s, s ^ 1) for s in range(sections)])

    def across(block, d, *pairs):
        route = [
            (s * spaces + i, t * spaces + (i + d) % spaces) for s, t in pairs for i in range(spaces)
        ]
        return lax.ppermute(block, BOTH, route)

    def hop(block, chip):
        pairs = [[(1, 2), (6, 5)], [(3, 4), (2, 1)], [(5, 6), (4, 3)]][chip]
        moved = {d: across(block, d, *pairs) for d in (2, -2, 1, -1, 0)}
        return [moved[d] for d in (2, 1, 0, -1, -2)]

    def halves(block):
        got = []
        for d in (2, 1):
            route = []
            for s in range(sections):
                move = d if s % 2 == 0 else -d
                route += [
                    (s * spaces + i, s * spaces + (i + move) % spaces) for i in range(spaces)
                ]
            got.append(lax.ppermute(block, BOTH, route))
        return got

    def along(block, *pairs):
        return lax.ppermute(block, "section", pairs)

    def after(value, *others):
        return lax.optimization_barrier((value, *others))[0]

    own = features.reshape(1, cells, ch)
    cot_own = cotangent.reshape(1, cells, ch)
    pair = call(pack_kernel, [own, cot_own], [(2, BF16)], 0)[0]
    got = halves(pair)
    other = [sibling(g) for g in got]
    act = [got[0], got[1], own, other[1], other[0]]
    cot = [other[0], other[1], cot_own, got[1], got[0]]

    base3 = side_part(1, half - 1, *act)
    deps = [base3]
    keeps3, keeps1 = [], []
    for k in range(chips):
        base = bias if k in (0, half // 2) else base3
        if k == 1:
            out3, keep3, act5 = forward(3, k, act, base, [first3])
        else:
            out3, keep3 = forward(3, k, act, base, deps=deps)
        in3 = sibling(out3)
        keeps3.append(keep3)
        deps = []
        if k == chips - 1:
            keep3 = sum(keeps3[1:], keeps3[0])
            fac_even = sibling(keep3)
        out1, keep1 = forward(1, k, [in3], base3, deps=deps)
        keeps1.append(keep1)
        if k == 0:
            first3 = out3
        if k + 1 < chips:
            act = hop(out1, k)
        if k == 1:
            moved3 = along(after(out3, keep1), (0, 7), (2, 5))
            moved5 = along(after(act5, keep1), (2, 6))
            base3 = side_part(half + 1, sections - 1, moved5, moved3)
        deps = [base3] if k == 1 else []
    keep1 = sum(keeps1[1:], keeps1[0])

    fac1 = keep1[:1]
    got = halves(jnp.where(core == 0, sibling(fac1), fac1))
    other = [sibling(g) for g in got]
    facs = [other[0], other[1], fac1, got[1], got[0], fac_even]
    act_own = jnp.where(core == 0, keep3[3:], keep1[1:])
    late = jnp.where(core == 0, moved5[2:3], moved3[1:2])
    side_own = jnp.where(section < half, own, jnp.where(section == half, act_own, late))
    joined = jnp.concatenate([act_own[0], side_own[0]], 1)
    blocks = jnp.transpose(joined.reshape(cells, spaces, -1), (1, 0, 2))
    blocks = lax.all_to_all(blocks, "space", 0, 0, tiled=True).reshape(spaces, cells, -1)
    fac_even, blocks = lax.optimization_barrier((fac_even, blocks))
    facs[5] = fac_even
    slopes5, slopes3, deps = [], [], []
    for k in reversed(range(chips)):
        more = []
        if k == 0:
            more = [moved_7_6, even3, sum(slopes5[1:], slopes5[0])]
        send, slope5, *extra = wide_back(k, cot, facs if k == chips - 1 else [facs], *more, deps=deps)
        if k == chips - 1:
            facs = extra[0]
        got = sibling(send)
        if k == 0:
            down = [(q, q - 1) for q in range(1, sections, 2)]
            evens = {d: across(extra[0], d, *down) for d in (3, -3, 6, -6)}
            opposite = across(extra[1], 8, *down)
            back = side_back(2, 3, after(old5, slope5), old3)
            from_next = across(back[1] + sibling(back[1]), 0, (3, 4), (2, 1))
            deps = [*evens.values(), opposite, back]
            sent, slope3 = narrow_back(k, got, keep3, old3, slope5, weight, deps=deps)
            continue
        more, deps = [], []
        if k == 1:
            more = [skip_narrow, moved_7_6]
        if k == 2:
            back = side_back(half + 1, sections - 1, slopes5[0] + slope5, slopes3[0])
            moved_7_6 = along(back, (7, 1), (6, 2))
            skip_narrow = along(back, (5, 2))
            deps = [back]
        sent, slope3 = narrow_back(k, got, keep3, *more, deps=deps)
        deps = []
        slopes5.append(slope5)
        slopes3.append(slope3)
        cot = hop(sent, {3: 0, 2: 2, 1: 1}[k])
        if k == 1:
            old5 = sum(slopes5[1:], slopes5[0])
            old3 = sum(slopes3[1:], slopes3[0])
            even3 = sibling(old3)
            zero = jnp.zeros_like(blocks[:1])
            lower = jnp.concatenate([zero, blocks[:-1]], 0)
            upper = jnp.concatenate([blocks[1:], zero], 0)
            shifted = jnp.stack([lower, blocks, upper])
            start = (place - 1) % spaces
            shifted = lax.dynamic_slice_in_dim(
                jnp.concatenate([shifted, shifted], 1), start, spaces, axis=1
            )
            shifted = jnp.transpose(shifted.reshape(3, spaces * cells, -1), (0, 2, 1))
            window = call(
                functools.partial(lambda r, i, *refs: window_kernel(r, *refs), row),
                [info, shifted],
                jax.ShapeDtypeStruct((27, shifted.shape[1], spaces * cells), BF16),
                0,
            )
            deps = [window]

    odds = {d: sibling(evens[d]) for d in evens}
    back_opposite = sibling(opposite)

    term = (sent[0] + jnp.where(section == 1, from_next, 0).astype(F32)).astype(BF16)
    width = ch // chips
    pieces = [term[:, j * width : (j + 1) * width] for j in range(chips)]
    piece = pieces[0]
    for j in (2, 1, 3):
        moved = along(pieces[j], (0, 2 * j), (1, 2 * j + 1))
        piece = jnp.where(chip == j, moved, piece)
    lower, upper = piece[:, : width // 2], piece[:, width // 2 :]
    moved = sibling(jnp.where(core == 0, upper, lower))
    grad_features = jnp.where(core == 0, lower, upper).astype(F32) + moved.astype(F32)

    even_pieces = [slope3, evens[-3], evens[-6], opposite, evens[6], evens[3]]
    odd_pieces = [slope5, odds[-3], odds[-6], back_opposite, odds[6], odds[3]]
    pieces = [*even_pieces, *odd_pieces]
    anywhere = pl.BlockSpec(memory_space=pltpu.HBM)
    grad_weight = pl.pallas_call(
        functools.partial(weight_grad_kernel, [len(even_pieces), len(odd_pieces)]),
        out_shape=jax.ShapeDtypeStruct((27, window.shape[1], ch), F32),
        in_specs=[smem] + [anywhere] * (1 + len(pieces)),
        out_specs=vmem,
        scratch_shapes=[
            pltpu.VMEM(window.shape, BF16),
            pltpu.VMEM((spaces, cells, ch), BF16),
            pltpu.SemaphoreType.DMA((3 + len(even_pieces),)),
        ],
        compiler_params=pltpu.CompilerParams(vmem_limit_bytes=24 * 2**20),
    )(info, far(window), *map(far, pieces))
    return (
        grad_features.reshape(1, depth, row, -1),
        jnp.transpose(grad_weight, (1, 0, 2))[None],
    )


def solution(mesh):
    return jax.shard_map(
        shards,
        mesh=mesh,
        in_specs=(
            P("space", None, None, None),
            P("section", None, None, None),
            P("section", None),
            P("space", None, None, None),
        ),
        out_specs=(P("space", None, None, "section"), P("section", "space", None, None)),
        check_vma=False,
    )
```
